256 devices in a mesh: batch: 2 (over x_hi), rows: 128 (over z, y, x_lo, core).
Axes of the slice: x: 4 (x_hi: 2, x_lo: 2; x = x_hi * 2 + x_lo), y: 4, z: 8, core: 2. Of those that a mesh axis runs over, the one named last changes fastest.
Arguments:
- surface: bfloat16 [2, 64, 2048, 1024], P('batch', None, 'rows'), may hold values from -6 to 6
- cotangent: bfloat16 [2, 64, 2048, 1024], P('batch', None, 'rows'), may hold values from -6 to 6
- spectral_weight: bfloat16 [256, 2, 64, 64, 128], P('rows', None, None, None, 'batch'), may hold values from -3 to 3
- local_weight: bfloat16 [64, 64], replicated, may hold values from -0.75 to 0.75
- bias_vector: float32 [64], replicated, may hold values from -1 to 1
Outputs:
- surface_gradient: bfloat16 [2, 64, 2048, 1024], P('batch', None, 'rows')
- weight_gradient: float32 [256, 2, 64, 64, 128], P('rows', None, None, None, 'batch')
The draws below stay inside these ranges and needn't reach their ends.
All inputs are finite; a program needn't handle non-finite values.
Results may differ from the reference program's by a relative error of at most 0.027.
Values may be sent and summed in bfloat16 or wider, within the bound.
A program may use at most 128 MiB of HBM per device.

```python
import math
import jax
import jax.numpy as jnp
from jax import lax

C = 64
KH = 128
KW = 256
COLS = 1024
HEIGHT = 2048
BATCH = 2


def levels(rng, shape, pieces, smallest, top_value):
    factor_of, own = 1.0, jax.random.fold_in(rng, 6)
    for axis_at, parts in pieces:
        steps = jnp.exp(jax.random.uniform(jax.random.fold_in(own, axis_at), (parts,), jnp.float32, smallest / len(pieces), top_value / len(pieces)))
        factor_of = factor_of * jnp.repeat(steps, shape[axis_at] // parts).reshape([-1 if axis == axis_at else 1 for axis in range(len(shape))])
    return factor_of


def scatter_about(key, shape, deviation, bound, shards=(), dtype=jnp.bfloat16):
    values = deviation * jax.random.normal(key, shape, jnp.float32)
    if shards:
        values = values * levels(key, shape, shards, -0.22, 0.18)
    return jnp.clip(values, -bound, bound).astype(dtype)


def setup_inputs(seed: int = 0) -> dict:
    key_of = jax.random.split(jax.random.key(seed), 6)
    return {
        "surface": scatter_about(key_of[0], (BATCH, C, HEIGHT, COLS), 1.0, 6.0, ((0, 2), (2, 128))),
        "cotangent": scatter_about(key_of[1], (BATCH, C, HEIGHT, COLS), 1.0, 6.0, ((0, 2), (2, 128))),
        "spectral_weight": scatter_about(key_of[2], (KW, 2, C, C, KH), (max(1, 4 * C * KH * KW // (HEIGHT * COLS))) ** -0.5, 3.0, ((0, 128), (4, 2))),
        "local_weight": scatter_about(key_of[3], (C, C), C ** -0.5, 0.75),
        "bias_vector": jnp.clip(jax.random.uniform(key_of[4], (C,), jnp.float32, -1.0, 1.0), -1.0, 1.0),
    }


def gelu_slope(argument):
    cumulative = 0.5 * (1.0 + jax.scipy.special.erf(argument * (1.0 / math.sqrt(2.0))))
    density = jnp.exp(-0.5 * argument * argument) * (1.0 / math.sqrt(2.0 * math.pi))
    return cumulative + argument * density

def rounded(argument):
    return lax.optimization_barrier(argument.astype(jnp.bfloat16)).astype(jnp.float32)

def row_index():
    lower_half = jnp.arange(KH // 2).astype(jnp.int32)
    upper_half = (HEIGHT - KH // 2 + jnp.arange(KH // 2)).astype(jnp.int32)
    return jnp.concatenate([lower_half, upper_half]).astype(jnp.int32)

def einsum_f32(pattern, left, right):
    return jnp.einsum(pattern, left.astype(jnp.float32), right.astype(jnp.float32))

def reference(surface, cotangent, spectral_weight, local_weight, bias_vector):
    channels_first = jnp.swapaxes(surface, 0, 1)
    cotangent_first = jnp.swapaxes(cotangent, 0, 1)
    surface_float = channels_first.astype(jnp.float32)
    doubling = jnp.where(jnp.arange(KW) == 0, 1.0, 2.0).astype(jnp.float32)
    scaling = 1.0 / (HEIGHT * COLS)
    picked = row_index()

    def column_spectrum(channel_plane):
        spectrum = jnp.fft.rfft(channel_plane.astype(jnp.float32), axis=-1)[..., :KW]
        return (jnp.real(spectrum).astype(jnp.bfloat16), jnp.imag(spectrum).astype(jnp.bfloat16))
    spec_real, spec_imag = lax.map(column_spectrum, channels_first)
    complex_cols = spec_real.astype(jnp.float32) + 1j * spec_imag.astype(jnp.float32)
    row_modes = jnp.fft.fft(complex_cols, axis=2)[:, :, picked, :]
    x_real = rounded(jnp.real(row_modes))
    x_imag = rounded(jnp.imag(row_modes))
    w_real = spectral_weight[:, 0]
    w_imag = spectral_weight[:, 1]
    forward_pattern = 'ibjk,kioj->objk'
    y_real = rounded(einsum_f32(forward_pattern, x_real, w_real) - einsum_f32(forward_pattern, x_imag, w_imag))
    y_imag = rounded(einsum_f32(forward_pattern, x_real, w_imag) + einsum_f32(forward_pattern, x_imag, w_real))
    placed = jnp.zeros_like(complex_cols).at[:, :, picked, :].set(y_real + 1j * y_imag)
    returned = jnp.fft.ifft(placed, axis=2) * HEIGHT
    b_real = jnp.real(returned).astype(jnp.bfloat16)
    b_imag = jnp.imag(returned).astype(jnp.bfloat16)

    def forward_plane(operands):
        real_part, imag_part, cotangent_plane, weight_column, offset = operands
        spectrum = real_part.astype(jnp.float32) + 1j * imag_part.astype(jnp.float32)
        padded = jnp.pad(spectrum, ((0, 0), (0, 0), (0, COLS // 2 + 1 - KW)))
        spectral_part = jnp.fft.irfft(padded, n=COLS, axis=-1) / HEIGHT
        local_part = jnp.einsum('ibhw,i->bhw', surface_float, weight_column.astype(jnp.float32))
        before = spectral_part + local_part + offset
        slopes = (cotangent_plane.astype(jnp.float32) * gelu_slope(before)).astype(jnp.bfloat16)
        slope_spec = jnp.fft.rfft(slopes.astype(jnp.float32), axis=-1)[..., :KW] * (doubling * scaling)
        return (slopes, jnp.real(slope_spec).astype(jnp.bfloat16), jnp.imag(slope_spec).astype(jnp.bfloat16))
    slopes_all, g_real, g_imag = lax.map(forward_plane, (b_real, b_imag, cotangent_first, jnp.swapaxes(local_weight, 0, 1), bias_vector))
    slope_cols = g_real.astype(jnp.float32) + 1j * g_imag.astype(jnp.float32)
    slope_modes = jnp.fft.fft(slope_cols, axis=2)[:, :, picked, :]
    gy_real = rounded(jnp.real(slope_modes))
    gy_imag = rounded(jnp.imag(slope_modes))
    grad_pattern = 'ibjk,objk->kioj'
    d_real = einsum_f32(grad_pattern, x_real, gy_real) + einsum_f32(grad_pattern, x_imag, gy_imag)
    d_imag = einsum_f32(grad_pattern, x_real, gy_imag) - einsum_f32(grad_pattern, x_imag, gy_real)
    weight_gradient = jnp.stack([d_real, d_imag], axis=1)
    back_pattern = 'objk,kioj->ibjk'
    in_real = rounded(einsum_f32(back_pattern, gy_real, w_real) + einsum_f32(back_pattern, gy_imag, w_imag))
    in_imag = rounded(einsum_f32(back_pattern, gy_imag, w_real) - einsum_f32(back_pattern, gy_real, w_imag))
    placed_grad = jnp.zeros_like(complex_cols).at[:, :, picked, :].set(in_real + 1j * in_imag)
    row_gradient = jnp.fft.ifft(placed_grad, axis=2) * HEIGHT
    r_real = jnp.real(row_gradient).astype(jnp.bfloat16)
    r_imag = jnp.imag(row_gradient).astype(jnp.bfloat16)
    slopes_float = slopes_all.astype(jnp.float32)

    def backward_plane(operands):
        real_part, imag_part, weight_row = operands
        spectrum = real_part.astype(jnp.float32) + 1j * imag_part.astype(jnp.float32)
        padded = jnp.pad(spectrum, ((0, 0), (0, 0), (0, COLS - KW)))
        spectral_grad = jnp.real(jnp.fft.ifft(padded, axis=-1)) * COLS
        local_grad = jnp.einsum('obhw,o->bhw', slopes_float, weight_row.astype(jnp.float32))
        return (spectral_grad + local_grad).astype(jnp.bfloat16)
    gradient_first = lax.map(backward_plane, (r_real, r_imag, local_weight))
    return (jnp.swapaxes(gradient_first, 0, 1), weight_gradient)
```

```python
import math

import jax
import jax.numpy as jnp
import numpy as np
from jax import lax
from jax.experimental import pallas as pl
from jax.experimental.pallas import tpu as pltpu
from jax.sharding import PartitionSpec as P

MESH = pl.DeviceIdType.MESH
BF = jnp.bfloat16
F32 = jnp.float32

C = 64
R = 16
W = 1024
KW = 256
KH = 128
NZ = 8
NQ = 16
NI = 4
ROWS = C * R
CHUNK = NQ * R


def tables():
    w = np.arange(W)[:, None]
    k = np.arange(KW)[None, :]
    angle = 2 * np.pi * ((w * k) % W) / W
    columns = np.concatenate([np.cos(angle), -np.sin(angle)], axis=1)
    height = NZ * NQ * R
    jj = np.arange(KH // 2)
    rows = np.zeros((NZ, 2 * CHUNK, 2 * KH))
    for z in range(NZ):
        h = (z * CHUNK + np.arange(CHUNK))[:, None]
        for half in range(2):
            f = (jj - half * (KH // 2))[None, :]
            angle = 2 * np.pi * ((f * h) % height) / height
            cos, sin = np.cos(angle), np.sin(angle)
            at = half * KH
            rows[z, :CHUNK, at : at + 64] = cos
            rows[z, :CHUNK, at + 64 : at + 128] = -sin
            rows[z, CHUNK:, at : at + 64] = sin
            rows[z, CHUNK:, at + 64 : at + 128] = cos
    return columns, rows


def permutations():
    gather = np.zeros((128, NI, NZ, 32))
    spread = np.zeros((128, 2, C))
    modes = np.zeros((NI, 32, NQ, NI, 2))
    for q in range(NQ):
        for i in range(NI):
            for kk in range(2):
                row = q * 8 + i * 2 + kk
                gather[row, i, :, 2 * q + kk] = 1
                spread[row, kk, 16 * i + q] = 1
                modes[i, 2 * q + kk, q, i, kk] = 1
    gather = gather.reshape(128, 1024)
    spread = spread.reshape(128, 128)
    return gather, spread, modes.reshape(128, 128), spread.T.copy()


def dot(a, b, ca=1, cb=0):
    return lax.dot_general(a, b, (((ca,), (cb,)), ((), ())), preferred_element_type=F32)


def gelu_slope(v):
    cumulative = 0.5 * (1.0 + lax.erf(v * (1.0 / math.sqrt(2.0))))
    density = jnp.exp(-0.5 * v * v) * (1.0 / math.sqrt(2.0 * math.pi))
    return cumulative + v * density


def expand_matrix(start):
    row = lax.broadcasted_iota(jnp.int32, (CHUNK, C), 0) + start
    col = lax.broadcasted_iota(jnp.int32, (CHUNK, C), 1)
    return (row // R == col).astype(F32).astype(BF)


def same_row_mask():
    row = lax.broadcasted_iota(jnp.int32, (CHUNK, CHUNK), 0) % R
    col = lax.broadcasted_iota(jnp.int32, (CHUNK, CHUNK), 1) % R
    return row == col


def mix_rows(weight_rows):
    mask = same_row_mask()
    for i in range(NI):
        spread = dot(weight_rows, expand_matrix(i * CHUNK), 1, 1)
        yield i, jnp.where(mask, spread, 0.0).astype(BF)


def column_scale():
    lane = lax.broadcasted_iota(jnp.int32, (1, KW), 1)
    return jnp.where(lane == 0, 2.0**-21, 2.0**-20).astype(F32)


def half_sign():
    lane = lax.broadcasted_iota(jnp.int32, (1, 128), 1)
    return jnp.where(lane < 64, -1.0, 1.0).astype(F32)


def transfers(
    x_hbm, cot_hbm, w_hbm, t1_hbm, t1t_hbm, rows_hbm, lw_ref, bias_ref, gather_ref, spread_ref, modes_ref, natural_ref,
    slopes_hbm, back_hbm, xm_hbm, gm_hbm,
    x, cot, w, t1, t1t, rt, w2r, w2i, kron, pre, slopes,
    a_out, a_in, b_out, b_in, c_out, c_in, d_out, d_in, e_out, e_in, f_out, f_in, turned, mixed, nat,
    load, store, sa, ra, sb, rb, sc, rc, sd, rd, se, re, sf, rf,
):
    b = lax.axis_index("batch")
    d = lax.axis_index("rows")
    z = d // NQ
    q = d % NQ

    def in_plane(p):
        return lax.rem(q + p, NQ)

    def along(p):
        return lax.rem(z + p, NZ)

    def wait(ref, sem):
        pltpu.make_async_copy(ref, ref, sem).wait()

    def send(src, dst, s, r, batch, row):
        pltpu.make_async_remote_copy(
            src_ref=src, dst_ref=dst, send_sem=s, recv_sem=r, device_id=(batch, row), device_id_type=MESH
        ).start()

    def loop(lo, hi, body):
        def step(p, carry):
            body(p)
            return carry

        lax.fori_loop(lo, hi, step, 0)

    loads = []
    for i in range(NI):
        part = pl.ds(i * CHUNK, CHUNK)
        loads.append(pltpu.make_async_copy(x_hbm.at[part], x.at[part], load.at[i]))
    load_t1 = pltpu.make_async_copy(t1_hbm, t1, load.at[4])
    load_rows = pltpu.make_async_copy(rows_hbm.at[z], rt, load.at[5])
    load_w = pltpu.make_async_copy(w_hbm, w, load.at[6])
    load_t1t = pltpu.make_async_copy(t1t_hbm, t1t, load.at[7])
    load_cot = pltpu.make_async_copy(cot_hbm, cot, load.at[8])
    load_t1.start()
    for copy in loads:
        copy.start()
    for copy in (load_rows, load_w, load_t1t, load_cot):
        copy.start()

    barrier = pltpu.get_barrier_semaphore()

    def greet(batch, row):
        pl.semaphore_signal(barrier, inc=1, device_id=(batch, row), device_id_type=MESH)

    loop(1, NQ, lambda p: greet(b, z * NQ + in_plane(p)))
    loop(0, NQ, lambda p: greet(1 - b, z * NQ + p))
    loop(1, NZ, lambda p: greet(b, along(p) * NQ + q))
    pl.semaphore_wait(barrier, 2 * NQ - 1 + NZ - 1)

    def send_plane(out, into, s, r, rnd, i):
        def one(p):
            to = in_plane(p)
            send(out.at[rnd, i, to], into.at[rnd, i, q], s.at[rnd, i], r.at[rnd, i], b, z * NQ + to)

        loop(1, NQ, one)
        pltpu.make_async_copy(out.at[rnd, i, q], into.at[rnd, i, q], r.at[rnd, i]).start()

    def send_owners(out, into, s, r, rnd):
        def same(p):
            to = in_plane(p)
            send(out.at[rnd, b, to], into.at[rnd, b, q], s.at[rnd, 0], r.at[rnd], b, z * NQ + to)

        def other(p):
            to = in_plane(p)
            send(out.at[rnd, 1 - b, to], into.at[rnd, b, q], s.at[rnd, 1], r.at[rnd], 1 - b, z * NQ + to)

        loop(0, NQ, other)
        loop(1, NQ, same)
        pltpu.make_async_copy(out.at[rnd, b, q], into.at[rnd, b, q], r.at[rnd]).start()

    def to_modes(rnd, i):
        wait(a_in.at[rnd, i], ra.at[rnd, i])
        plane = a_in[rnd, i].reshape(CHUNK, 2 * KW)
        term = dot(plane[:, :KW], rt[:CHUNK], 0, 0) + dot(plane[:, KW:], rt[CHUNK:], 0, 0)
        b_out[rnd, i] = term.astype(BF).reshape(NZ, 32, 2 * KH)

        def one(p):
            to = along(p)
            send(b_out.at[rnd, i, to], b_in.at[rnd, i, z], sb.at[rnd, i], rb.at[rnd], b, to * NQ + q)

        loop(1, NZ, one)
        pltpu.make_async_copy(b_out.at[rnd, i, z], b_in.at[rnd, i, z], rb.at[rnd]).start()

    def to_owners(rnd):
        wait(b_in.at[rnd], rb.at[rnd])
        total = dot(gather_ref[...], b_in[rnd].reshape(1024, 2 * KH))
        for half in range(2):
            c_out[rnd, half] = total[:, half * KH : (half + 1) * KH].reshape(NQ, 8, KH)
        send_owners(c_out, c_in, sc, rc, rnd)

    def from_owners(rnd):
        for m in range(2):
            d_out[rnd, m] = dot(spread_ref[...], mixed[m].astype(BF)).reshape(NQ, 8, KH)
        send_owners(d_out, d_in, sd, rd, rnd)
        wait(d_in.at[rnd], rd.at[rnd])
        halves = [dot(modes_ref[...], d_in[rnd, half].reshape(128, KH).astype(BF)) for half in range(2)]
        e_out[rnd] = jnp.concatenate(halves, axis=1).astype(BF).reshape(NI, 32, 2 * KH)

        def spread_modes(i):
            def one(p):
                send(e_out.at[rnd, i], e_in.at[rnd, i, z], se.at[rnd, i], re.at[rnd, i], b, along(p) * NQ + q)

            loop(1, NZ, one)
            pltpu.make_async_copy(e_out.at[rnd, i], e_in.at[rnd, i, z], re.at[rnd, i]).start()

        loop(0, NI, spread_modes)

        def to_rows(i):
            wait(e_in.at[rnd, i], re.at[rnd, i])
            spectra = e_in[rnd, i].reshape(KW, 2 * KH)
            real = dot(rt[:CHUNK], spectra, 1, 1)
            imag = dot(rt[CHUNK:], spectra, 1, 1)
            if rnd == 0:
                real = real * column_scale()
                imag = imag * column_scale()
            f_out[rnd, i] = jnp.concatenate([real, imag], axis=1).astype(BF).reshape(NQ, R, 2 * KW)
            send_plane(f_out, f_in, sf, rf, rnd, i)

        loop(0, NI, to_rows)

    load_t1.wait()

    def first(i):
        part = pl.ds(pl.multiple_of(i * CHUNK, CHUNK), CHUNK)
        pltpu.make_async_copy(x_hbm.at[part], x.at[part], load.at[i]).wait()
        a_out[0, i] = dot(x[part], t1[...]).astype(BF).reshape(NQ, R, 2 * KW)
        send_plane(a_out, a_in, sa, ra, 0, i)

    loop(0, NI, first)
    load_w.wait()

    def widen(c):
        for kk in range(2):
            for part, wide in enumerate((w2r, w2i)):
                block = w[kk, part, c].astype(F32)
                wide[kk, c] = jnp.concatenate([block, block], axis=1)

    loop(0, C, widen)
    load_rows.wait()
    loop(0, NI, lambda i: to_modes(0, i))

    def pointwise(n):
        start = pl.multiple_of(n * CHUNK, CHUNK)
        mine = expand_matrix(start)
        rows_of = dot(mine, lw_ref[...], 1, 1).astype(BF)
        for i, block in mix_rows(rows_of):
            kron[:, i * CHUNK : (i + 1) * CHUNK] = block
        offset = jnp.sum(mine.astype(F32) * bias_ref[...], axis=1, keepdims=True)
        pre[pl.ds(start, CHUNK)] = dot(kron[...], x[...]) + offset

    loop(0, NI, pointwise)
    to_owners(0)

    def turn(rnd):
        for m in range(2):
            rows_of = c_in[rnd, m].reshape(128, KH)
            turned[m] = (pltpu.roll(rows_of, 64, 1) * half_sign()).reshape(NQ, 8, KH)

    wait(c_in.at[0], rc.at[0])
    turn(0)
    for kk in range(2):

        def mix(qq, sums):
            sums = list(sums)
            for i in range(NI):
                real = w2r[kk, 16 * i + qq]
                imag = w2i[kk, 16 * i + qq]
                for m in range(2):
                    row = 2 * i + kk
                    sums[m] = sums[m] + c_in[0, m, qq, row : row + 1] * real + turned[m, qq, row : row + 1] * imag
            return tuple(sums)

        sums = lax.fori_loop(0, NQ, mix, (jnp.zeros((C, KH), F32),) * 2)
        for m in range(2):
            mixed[m, kk * C : (kk + 1) * C] = sums[m]
    copy_xm = pltpu.make_async_copy(c_in.at[0], xm_hbm, store.at[NI])
    copy_xm.start()
    from_owners(0)

    load_t1t.wait()
    load_cot.wait()

    def second(i):
        start = pl.multiple_of(i * CHUNK, CHUNK)
        part = pl.ds(start, CHUNK)
        wait(f_in.at[0, i], rf.at[0, i])
        pre[part] += dot(f_in[0, i].reshape(CHUNK, 2 * KW), t1t[...])

        def slab(s):
            at = pl.ds(pl.multiple_of(start + s * 16, 16), 16)
            slopes[at] = (cot[at].astype(F32) * gelu_slope(pre[at])).astype(BF)

        loop(0, CHUNK // 16, slab)
        pltpu.make_async_copy(slopes.at[part], slopes_hbm.at[part], store.at[i]).start()
        scale = jnp.concatenate([column_scale()] * 2, axis=1)
        a_out[1, i] = (dot(slopes[part], t1[...]) * scale).astype(BF).reshape(NQ, R, 2 * KW)
        send_plane(a_out, a_in, sa, ra, 1, i)

    loop(0, NI, second)
    loop(0, NI, lambda i: to_modes(1, i))
    to_owners(1)
    wait(c_in.at[1], rc.at[1])
    for m in range(2):
        nat[m] = dot(natural_ref[...], c_in[1, m].reshape(128, KH).astype(BF))
        turned[m] = (pltpu.roll(nat[m], 64, 1) * -half_sign()).reshape(NQ, 8, KH)
    copy_gm = pltpu.make_async_copy(nat, gm_hbm, store.at[NI + 1])
    copy_gm.start()
    for kk in range(2):
        at = slice(kk * C, (kk + 1) * C)
        grads = [nat[m, at] for m in range(2)]
        grads_turned = [turned[m].reshape(128, KH)[at] for m in range(2)]

        def mix_back(c8):
            rows_of = ([], [])
            for n in range(8):
                c = c8 * 8 + n
                real = w2r[kk, c]
                imag = w2i[kk, c]
                for m in range(2):
                    rows_of[m].append(jnp.sum(grads[m] * real + grads_turned[m] * imag, axis=0, keepdims=True))
            for m in range(2):
                mixed[m, pl.ds(pl.multiple_of(kk * C + c8 * 8, 8), 8)] = jnp.concatenate(rows_of[m], axis=0)

        loop(0, C // 8, mix_back)
    from_owners(1)

    def last(i):
        wait(f_in.at[1, i], rf.at[1, i])
        part = pl.ds(pl.multiple_of(i * NQ, NQ), NQ)
        pltpu.make_async_copy(f_in.at[1, i], back_hbm.at[part], store.at[NI + 2 + i]).start()

    loop(0, NI, last)

    for i in range(NI):
        part = pl.ds(i * CHUNK, CHUNK)
        pltpu.make_async_copy(slopes.at[part], slopes_hbm.at[part], store.at[i]).wait()
        pltpu.make_async_copy(f_in.at[1, i], back_hbm.at[pl.ds(i * NQ, NQ)], store.at[NI + 2 + i]).wait()
    copy_xm.wait()
    copy_gm.wait()
    for rnd in range(2):
        for i in range(NI):
            wait(a_out.at[rnd, i, pl.ds(0, NQ - 1)], sa.at[rnd, i])
            wait(f_out.at[rnd, i, pl.ds(0, NQ - 1)], sf.at[rnd, i])
            wait(b_out.at[rnd, i, pl.ds(0, NZ - 1)], sb.at[rnd, i])
            wait(e_in.at[rnd, i, pl.ds(0, NZ - 1)], se.at[rnd, i])
        for out, s in ((c_out, sc), (d_out, sd)):
            wait(out.at[rnd, 0, pl.ds(0, NQ - 1)], s.at[rnd, 0])
            wait(out.at[rnd, 0], s.at[rnd, 1])


def outputs(
    slopes, back, t1t, lw, xm, gm, sg_hbm, wg_hbm,
    kron, sg, wg, xr, xi, turned, store_s, store_w,
):
    for m in range(2):
        rows_of = xm[m].reshape(128, KH)
        swapped = pltpu.roll(rows_of, 64, 1)
        low = lax.broadcasted_iota(jnp.int32, (128, KH), 1) < 64
        xr[m] = jnp.where(low, rows_of, swapped).reshape(NQ, 8, KH)
        xi[m] = jnp.where(low, swapped, rows_of).reshape(NQ, 8, KH)
        turned[m] = pltpu.roll(gm[m], 64, 1) * -half_sign()
    for kk in range(2):
        at = slice(kk * C, (kk + 1) * C)
        for i in range(NI):

            def term(qq, carry):
                row = 2 * i + kk
                total = jnp.zeros((C, KH), F32)
                for m in range(2):
                    total = total + xr[m, qq, row : row + 1] * gm[m, at] + xi[m, qq, row : row + 1] * turned[m, at]
                wg[kk, 0, 16 * i + qq] = total[:, :64]
                wg[kk, 1, 16 * i + qq] = total[:, 64:]
                return carry

            lax.fori_loop(0, NQ, term, 0)
        pltpu.make_async_copy(wg.at[kk], wg_hbm.at[kk], store_w.at[kk]).start()

    def surface_part(n, carry):
        start = pl.multiple_of(n * CHUNK, CHUNK)
        rows_of = dot(expand_matrix(start), lw[...]).astype(BF)
        for i, block in mix_rows(rows_of):
            kron[:, i * CHUNK : (i + 1) * CHUNK] = block
        part = pl.ds(start, CHUNK)
        sg[part] = (dot(kron[...], slopes[...]) + dot(back[part], t1t[...])).astype(BF)
        pltpu.make_async_copy(sg.at[part], sg_hbm.at[part], store_s.at[n]).start()
        return carry

    lax.fori_loop(0, NI, surface_part, 0)
    for n in range(NI):
        part = pl.ds(n * CHUNK, CHUNK)
        pltpu.make_async_copy(sg.at[part], sg_hbm.at[part], store_s.at[n]).wait()
    for kk in range(2):
        pltpu.make_async_copy(wg.at[kk], wg_hbm.at[kk], store_w.at[kk]).wait()


def local(surface, cotangent, spectral_weight, local_weight, bias_vector):
    columns, rows = tables()
    t1 = jnp.asarray(columns, BF)
    t1t = jnp.asarray(columns.T, BF)
    row_table = jnp.asarray(rows, BF)
    gather, spread, modes, natural = (jnp.asarray(p, BF) for p in permutations())
    anywhere = pl.BlockSpec(memory_space=pl.ANY)
    vmem = pl.BlockSpec(memory_space=pltpu.VMEM)
    DMA = pltpu.SemaphoreType.DMA
    V = pltpu.VMEM
    shape = jax.ShapeDtypeStruct
    slopes, back, xm, gm = pl.pallas_call(
        transfers,
        out_shape=(
            shape((ROWS, W), BF),
            shape((C, R, 2 * KW), BF),
            shape((2, NQ, 8, KH), F32),
            shape((2, 128, KH), F32),
        ),
        in_specs=[anywhere] * 6 + [vmem] * 6,
        out_specs=[anywhere] * 4,
        scratch_shapes=[
            V((ROWS, W), BF),
            V((ROWS, W), BF),
            V((2, 2, C, C, 64), BF),
            V((W, 2 * KW), BF),
            V((2 * KW, W), BF),
            V((2 * CHUNK, 2 * KH), BF),
            V((2, C, C, KH), F32),
            V((2, C, C, KH), F32),
            V((CHUNK, ROWS), BF),
            V((ROWS, W), F32),
            V((ROWS, W), BF),
            V((2, NI, NQ, R, 2 * KW), BF),
            V((2, NI, NQ, R, 2 * KW), BF),
            V((2, NI, NZ, 32, 2 * KH), BF),
            V((2, NI, NZ, 32, 2 * KH), BF),
            V((2, 2, NQ, 8, KH), F32),
            V((2, 2, NQ, 8, KH), F32),
            V((2, 2, NQ, 8, KH), F32),
            V((2, 2, NQ, 8, KH), F32),
            V((2, NI, 32, 2 * KH), BF),
            V((2, NI, NZ, 32, 2 * KH), BF),
            V((2, NI, NQ, R, 2 * KW), BF),
            V((2, NI, NQ, R, 2 * KW), BF),
            V((2, NQ, 8, KH), F32),
            V((2, 128, KH), F32),
            V((2, 128, KH), F32),
            DMA((9,)),
            DMA((NI + 2 + NI,)),
            DMA((2, NI)),
            DMA((2, NI)),
            DMA((2, NI)),
            DMA((2,)),
            DMA((2, 2)),
            DMA((2,)),
            DMA((2, 2)),
            DMA((2,)),
            DMA((2, NI)),
            DMA((2, NI)),
            DMA((2, NI)),
            DMA((2, NI)),
        ],
        compiler_params=pltpu.CompilerParams(
            collective_id=0, has_side_effects=True, vmem_limit_bytes=56 * 1024 * 1024
        ),
        name="transfers",
    )(
        surface.reshape(ROWS, W),
        cotangent.reshape(ROWS, W),
        spectral_weight,
        t1,
        t1t,
        row_table,
        local_weight,
        bias_vector.reshape(1, C),
        gather,
        spread,
        modes,
        natural,
    )
    surface_gradient, weight_gradient = pl.pallas_call(
        outputs,
        out_shape=(shape((ROWS, W), BF), shape((2, 2, C, C, 64), F32)),
        in_specs=[vmem] * 6,
        out_specs=[anywhere] * 2,
        scratch_shapes=[
            V((CHUNK, ROWS), BF),
            V((ROWS, W), BF),
            V((2, 2, C, C, 64), F32),
            V((2, NQ, 8, KH), F32),
            V((2, NQ, 8, KH), F32),
            V((2, 128, KH), F32),
            DMA((NI,)),
            DMA((2,)),
        ],
        compiler_params=pltpu.CompilerParams(vmem_limit_bytes=48 * 1024 * 1024),
        name="outputs",
    )(slopes, back.reshape(ROWS, 2 * KW), t1t, local_weight, xm, gm)
    return surface_gradient.reshape(1, C, R, W), weight_gradient


def solution(mesh):
    placed = (
        P("batch", None, "rows", None),
        P("batch", None, "rows", None),
        P("rows", None, None, None, "batch"),
        P(),
        P(),
    )
    return jax.shard_map(
        local,
        mesh=mesh,
        in_specs=placed,
        out_specs=(P("batch", None, "rows", None), P("rows", None, None, None, "batch")),
        check_vma=False,
    )
```

```python
import math

import jax
import jax.numpy as jnp
import numpy as np
from jax import lax
from jax.experimental import pallas as pl
from jax.experimental.pallas import tpu as pltpu
from jax.sharding import PartitionSpec as P

MESH = pl.DeviceIdType.MESH
BF = jnp.bfloat16
F32 = jnp.float32

C = 64
R = 16
W = 1024
KW = 256
KO = KW // 2
KH = 128
NZ = 8
NQ = 16
NI = 4
ROWS = C * R
CHUNK = NQ * R


def tables():
    w = np.arange(W)[:, None]
    columns = []
    for kk in range(2):
        k = 2 * np.arange(KO)[None, :] + kk
        angle = 2 * np.pi * ((w * k) % W) / W
        columns += [np.cos(angle), -np.sin(angle)]
    columns = np.concatenate(columns, axis=1)
    height = NZ * NQ * R
    jj = np.arange(KH // 2)
    rows = np.zeros((NZ, 2 * CHUNK, 2 * KH))
    for z in range(NZ):
        h = (z * CHUNK + np.arange(CHUNK))[:, None]
        for half in range(2):
            f = (jj - half * (KH // 2))[None, :]
            angle = 2 * np.pi * ((f * h) % height) / height
            cos, sin = np.cos(angle), np.sin(angle)
            at = half * KH
            rows[z, :CHUNK, at : at + 64] = cos
            rows[z, :CHUNK, at + 64 : at + 128] = -sin
            rows[z, CHUNK:, at : at + 64] = sin
            rows[z, CHUNK:, at + 64 : at + 128] = cos
    return columns, rows


def permutations():
    gather = np.zeros((NQ, NI, NI, NZ, NQ))
    spread = np.zeros((NQ, NI, C))
    for q in range(NQ):
        for i in range(NI):
            gather[q, i, i, :, q] = 1
            spread[q, i, 16 * i + q] = 1
    gather = gather.reshape(64, 512)
    spread = spread.reshape(64, 64)
    return gather, spread, spread.T.copy()


def dot(a, b, ca=1, cb=0):
    return lax.dot_general(a, b, (((ca,), (cb,)), ((), ())), preferred_element_type=F32)


def gelu_slope(v):
    cumulative = 0.5 * (1.0 + lax.erf(v * (1.0 / math.sqrt(2.0))))
    density = jnp.exp(-0.5 * v * v) * (1.0 / math.sqrt(2.0 * math.pi))
    return cumulative + v * density


def expand_matrix(start):
    row = lax.broadcasted_iota(jnp.int32, (CHUNK, C), 0) + start
    col = lax.broadcasted_iota(jnp.int32, (CHUNK, C), 1)
    return (row // R == col).astype(F32).astype(BF)


def same_row_mask():
    row = lax.broadcasted_iota(jnp.int32, (CHUNK, CHUNK), 0) % R
    col = lax.broadcasted_iota(jnp.int32, (CHUNK, CHUNK), 1) % R
    return row == col


def mix_rows(weight_rows):
    mask = same_row_mask()
    for i in range(NI):
        spread = dot(weight_rows, expand_matrix(i * CHUNK), 1, 1)
        yield i, jnp.where(mask, spread, 0.0).astype(BF)


def column_scale(kk):
    if kk:
        return jnp.full((1, 2 * KO), 2.0**-20, F32)
    lane = lax.broadcasted_iota(jnp.int32, (1, 2 * KO), 1)
    return jnp.where(lane % KO == 0, 2.0**-21, 2.0**-20).astype(F32)


def half_sign():
    lane = lax.broadcasted_iota(jnp.int32, (1, 128), 1)
    return jnp.where(lane < 64, -1.0, 1.0).astype(F32)


def transfers(
    x_hbm, cot_hbm, w_hbm, t1_hbm, t1t_hbm, rows_hbm, lw_ref, bias_ref, gather_ref, spread_ref, natural_ref,
    sg_hbm, xm_hbm, gm_hbm,
    x, cot, w, t1, t1t, rt, w2r, w2i, kron, pre, slopes,
    a_out, a_in, b_out, b_in, c_out, c_in, d_out, d_in, e_out, e_in, f_out, f_in, turned, mixed, nat,
    load, store, sa, ra, sb, rb, sc, rc, sd, rd, se, re, sf, rf,
):
    b = lax.axis_index("batch")
    d = lax.axis_index("rows")
    z = d // NQ
    q = d % NQ

    def in_plane(p):
        return lax.rem(q + p, NQ)

    def along(p):
        return lax.rem(z + p, NZ)

    def wait(ref, sem):
        pltpu.make_async_copy(ref, ref, sem).wait()

    def send(src, dst, s, r, batch, row):
        pltpu.make_async_remote_copy(
            src_ref=src, dst_ref=dst, send_sem=s, recv_sem=r, device_id=(batch, row), device_id_type=MESH
        ).start()

    def loop(lo, hi, body):
        def step(p, carry):
            body(p)
            return carry

        lax.fori_loop(lo, hi, step, 0)

    barrier = pltpu.get_barrier_semaphore()

    def greet(batch, row):
        pl.semaphore_signal(barrier, inc=1, device_id=(batch, row), device_id_type=MESH)

    loads = []
    for i in range(NI):
        part = pl.ds(i * CHUNK, CHUNK)
        loads.append(pltpu.make_async_copy(x_hbm.at[part], x.at[part], load.at[i]))
    load_t1 = pltpu.make_async_copy(t1_hbm, t1, load.at[4])
    load_rows = pltpu.make_async_copy(rows_hbm.at[z], rt, load.at[5])
    load_w = pltpu.make_async_copy(w_hbm, w, load.at[6])
    load_t1t = pltpu.make_async_copy(t1t_hbm, t1t, load.at[7])
    load_cot = pltpu.make_async_copy(cot_hbm, cot, load.at[8])
    load_t1.start()
    for copy in loads:
        copy.start()
    loop(1, NQ, lambda p: greet(b, z * NQ + in_plane(p)))
    loop(0, NQ, lambda p: greet(1 - b, z * NQ + p))
    loop(1, NZ, lambda p: greet(b, along(p) * NQ + q))
    for copy in (load_rows, load_w, load_t1t, load_cot):
        copy.start()

    def split_columns(rnd, i, rows_of):
        field = dot(rows_of, t1[...])
        for kk in range(2):
            half = field[:, kk * 256 : (kk + 1) * 256]
            if rnd:
                half = half * column_scale(kk)
            a_out[rnd, kk, i] = half.astype(BF).reshape(NQ, R, 256)

    load_t1.wait()

    def first(i):
        part = pl.ds(pl.multiple_of(i * CHUNK, CHUNK), CHUNK)
        pltpu.make_async_copy(x_hbm.at[part], x.at[part], load.at[i]).wait()
        split_columns(0, i, x[part])

    loop(0, NI, first)
    pl.semaphore_wait(barrier, 2 * NQ - 1 + NZ - 1)

    def send_plane(out, into, s, r, rnd, kk, i):
        def one(p):
            to = in_plane(p)
            send(
                out.at[rnd, kk, i, to], into.at[rnd, kk, i, q], s.at[rnd, kk, i], r.at[rnd, kk, i], b, z * NQ + to
            )

        loop(1, NQ, one)
        pltpu.make_async_copy(out.at[rnd, kk, i, q], into.at[rnd, kk, i, q], r.at[rnd, kk, i]).start()

    def sent_plane(out, s, rnd, kk, i):
        wait(out.at[rnd, kk, i, pl.ds(0, NQ - 1)], s.at[rnd, kk, i])

    def send_owners(out, into, s, r, rnd, kk):
        def same(p):
            to = in_plane(p)
            send(
                out.at[rnd, kk, b, to], into.at[rnd, kk, b, q], s.at[rnd, kk, 0], r.at[rnd, kk], b, z * NQ + to
            )

        def other(p):
            to = in_plane(p)
            send(
                out.at[rnd, kk, 1 - b, to], into.at[rnd, kk, b, q], s.at[rnd, kk, 1], r.at[rnd, kk], 1 - b, z * NQ + to
            )

        loop(0, NQ, other)
        loop(1, NQ, same)
        pltpu.make_async_copy(out.at[rnd, kk, b, q], into.at[rnd, kk, b, q], r.at[rnd, kk]).start()

    def to_modes(rnd, kk):
        def one_channel(i):
            wait(a_in.at[rnd, kk, i], ra.at[rnd, kk, i])
            plane = a_in[rnd, kk, i].reshape(CHUNK, 2 * KO)
            term = dot(plane[:, :KO], rt[:CHUNK], 0, 0) + dot(plane[:, KO:], rt[CHUNK:], 0, 0)
            b_out[rnd, kk, i] = term.astype(BF).reshape(NZ, NQ, 2 * KH)

            def one(p):
                to = along(p)
                send(
                    b_out.at[rnd, kk, i, to], b_in.at[rnd, kk, i, z], sb.at[rnd, kk, i], rb.at[rnd, kk], b, to * NQ + q
                )

            loop(1, NZ, one)
            pltpu.make_async_copy(b_out.at[rnd, kk, i, z], b_in.at[rnd, kk, i, z], rb.at[rnd, kk]).start()

        loop(0, NI, one_channel)

    def to_owners(rnd, kk):
        wait(b_in.at[rnd, kk], rb.at[rnd, kk])
        total = dot(gather_ref[...], b_in[rnd, kk].reshape(512, 2 * KH))
        for half in range(2):
            c_out[rnd, kk, half] = total[:, half * KH : (half + 1) * KH].reshape(NQ, NI, KH)
        send_owners(c_out, c_in, sc, rc, rnd, kk)

    def from_owners(rnd, kk):
        for m in range(2):
            d_out[rnd, kk, m] = dot(spread_ref[...], mixed[m].astype(BF)).reshape(NQ, NI, KH)
        send_owners(d_out, d_in, sd, rd, rnd, kk)

    def spread_modes(rnd, kk):
        wait(d_in.at[rnd, kk], rd.at[rnd, kk])
        halves = [dot(natural_ref[...], d_in[rnd, kk, half].reshape(C, KH).astype(BF)) for half in range(2)]
        e_out[rnd, kk] = jnp.concatenate(halves, axis=1).astype(BF).reshape(NI, NQ, 2 * KH)

        def one_channel(i):
            def one(p):
                to = along(p)
                send(e_out.at[rnd, kk, i], e_in.at[rnd, kk, i, z], se.at[rnd, kk, i], re.at[rnd, kk, i], b, to * NQ + q)

            loop(1, NZ, one)
            pltpu.make_async_copy(e_out.at[rnd, kk, i], e_in.at[rnd, kk, i, z], re.at[rnd, kk, i]).start()

        loop(0, NI, one_channel)

    def to_rows(rnd, kk, lo=0, hi=NI):
        def one_channel(i):
            wait(e_in.at[rnd, kk, i], re.at[rnd, kk, i])
            both = dot(rt[...], e_in[rnd, kk, i].reshape(KO, 2 * KH), 1, 1)
            both = jnp.concatenate([both[:CHUNK], both[CHUNK:]], axis=1)
            if rnd == 0:
                both = both * column_scale(kk)
            f_out[rnd, kk, i] = both.astype(BF).reshape(NQ, R, 2 * KO)
            send_plane(f_out, f_in, sf, rf, rnd, kk, i)

        loop(lo, hi, one_channel)

    def from_rows(rnd, i):
        start = pl.multiple_of(i * CHUNK, CHUNK)
        total = pre[pl.ds(start, CHUNK)]
        for kk in range(2):
            wait(f_in.at[rnd, kk, i], rf.at[rnd, kk, i])
            total = total + dot(f_in[rnd, kk, i].reshape(CHUNK, 2 * KO), t1t[kk * 256 : (kk + 1) * 256])
        return total

    def pointwise(rnd, lo, hi):
        field, over = ((x, 1), (slopes, 0))[rnd]

        def rows_of_one(n):
            start = pl.multiple_of(n * CHUNK, CHUNK)
            mine = expand_matrix(start)
            for i, block in mix_rows(dot(mine, lw_ref[...], 1, over).astype(BF)):
                kron[:, i * CHUNK : (i + 1) * CHUNK] = block
            part = pl.ds(start, CHUNK)
            pre[part] = dot(kron[...], field[...])
            if rnd == 0:
                pre[part] += jnp.sum(mine.astype(F32) * bias_ref[...], axis=1, keepdims=True)

        loop(lo, hi, rows_of_one)

    def widen(c):
        for kk in range(2):
            for part, wide in enumerate((w2r, w2i)):
                block = w[kk, part, c].astype(F32)
                wide[kk, c] = jnp.concatenate([block, block], axis=1)

    def mix(kk):
        wait(c_in.at[0, kk], rc.at[0, kk])
        for m in range(2):
            rows_of = c_in[0, kk, m].reshape(C, KH)
            turned[m] = (pltpu.roll(rows_of, 64, 1) * half_sign()).reshape(NQ, NI, KH)

        def terms(qq, sums):
            sums = list(sums)
            for i in range(NI):
                real = w2r[kk, 16 * i + qq]
                imag = w2i[kk, 16 * i + qq]
                for m in range(2):
                    sums[m] = sums[m] + c_in[0, kk, m, qq, i : i + 1] * real + turned[m, qq, i : i + 1] * imag
            return tuple(sums)

        sums = lax.fori_loop(0, NQ, terms, (jnp.zeros((C, KH), F32),) * 2)
        for m in range(2):
            mixed[m] = sums[m]

    def mix_back(kk):
        wait(c_in.at[1, kk], rc.at[1, kk])
        grads = []
        grads_turned = []
        for m in range(2):
            grads.append(dot(natural_ref[...], c_in[1, kk, m].reshape(C, KH).astype(BF)))
            grads_turned.append(pltpu.roll(grads[m], 64, 1) * -half_sign())
            nat[kk, m] = grads[m]

        def terms(c8):
            rows_of = ([], [])
            for n in range(8):
                c = c8 * 8 + n
                real = w2r[kk, c]
                imag = w2i[kk, c]
                for m in range(2):
                    rows_of[m].append(jnp.sum(grads[m] * real + grads_turned[m] * imag, axis=0, keepdims=True))
            for m in range(2):
                mixed[m, pl.ds(pl.multiple_of(c8 * 8, 8), 8)] = jnp.concatenate(rows_of[m], axis=0)

        loop(0, C // 8, terms)

    for i in range(NI):
        send_plane(a_out, a_in, sa, ra, 0, 0, i)
    load_w.wait()
    loop(0, 24, widen)
    for i in range(NI):
        sent_plane(a_out, sa, 0, 0, i)
        send_plane(a_out, a_in, sa, ra, 0, 1, i)
        if i < 2:
            pointwise(0, i, i + 1)
    load_rows.wait()
    to_modes(0, 0)
    loop(24, 40, widen)
    to_modes(0, 1)
    to_owners(0, 0)
    loop(40, C, widen)
    to_owners(0, 1)
    mix(0)
    from_owners(0, 0)
    pointwise(0, 2, 3)
    mix(1)
    from_owners(0, 1)
    pointwise(0, 3, 4)
    spread_modes(0, 0)
    to_rows(0, 0, 0, 2)
    spread_modes(0, 1)
    to_rows(0, 0, 2, 4)
    to_rows(0, 1)
    copy_xm = pltpu.make_async_copy(c_in.at[0], xm_hbm, store.at[NI])
    copy_xm.start()

    load_t1t.wait()
    load_cot.wait()

    def second(i):
        start = pl.multiple_of(i * CHUNK, CHUNK)
        part = pl.ds(start, CHUNK)
        pre[part] = from_rows(0, i)

        def slab(s):
            at = pl.ds(pl.multiple_of(start + s * 16, 16), 16)
            slopes[at] = (cot[at].astype(F32) * gelu_slope(pre[at])).astype(BF)

        loop(0, CHUNK // 16, slab)
        split_columns(1, i, slopes[part])
        send_plane(a_out, a_in, sa, ra, 1, 0, i)

    loop(0, NI, second)
    for i in range(NI):
        send_plane(a_out, a_in, sa, ra, 1, 1, i)
    to_modes(1, 0)
    to_modes(1, 1)
    to_owners(1, 0)
    pointwise(1, 0, 2)
    to_owners(1, 1)
    mix_back(0)
    from_owners(1, 0)
    pointwise(1, 2, 3)
    mix_back(1)
    from_owners(1, 1)
    pointwise(1, 3, 4)
    spread_modes(1, 0)
    to_rows(1, 0, 0, 2)
    spread_modes(1, 1)
    to_rows(1, 0, 2, 4)
    to_rows(1, 1)
    copy_gm = pltpu.make_async_copy(nat, gm_hbm, store.at[NI + 1])
    copy_gm.start()

    def last(i):
        part = pl.ds(pl.multiple_of(i * CHUNK, CHUNK), CHUNK)
        x[part] = from_rows(1, i).astype(BF)
        pltpu.make_async_copy(x.at[part], sg_hbm.at[part], store.at[i]).start()

    loop(0, NI, last)

    for i in range(NI):
        part = pl.ds(i * CHUNK, CHUNK)
        pltpu.make_async_copy(x.at[part], sg_hbm.at[part], store.at[i]).wait()
    copy_xm.wait()
    copy_gm.wait()
    for rnd in range(2):
        for kk in range(2):

            def ended(i):
                sent_plane(f_out, sf, rnd, kk, i)
                wait(b_out.at[rnd, kk, i, pl.ds(0, NZ - 1)], sb.at[rnd, kk, i])
                wait(e_in.at[rnd, kk, i, pl.ds(0, NZ - 1)], se.at[rnd, kk, i])
                if rnd or kk:
                    sent_plane(a_out, sa, rnd, kk, i)

            loop(0, NI, ended)
            for out, s in ((c_out, sc), (d_out, sd)):
                wait(out.at[rnd, kk, 0, pl.ds(0, NQ - 1)], s.at[rnd, kk, 0])
                wait(out.at[rnd, kk, 0], s.at[rnd, kk, 1])


def outputs(sg_in, xm, gm, sg_hbm, wg_hbm, sg, wg, xr, xi, turned, load, store_s, store_w):
    loads, passes = [], []
    for n in range(NI):
        part = pl.ds(n * CHUNK, CHUNK)
        loads.append(pltpu.make_async_copy(sg_in.at[part], sg.at[part], load.at[n]))
        passes.append(pltpu.make_async_copy(sg.at[part], sg_hbm.at[part], store_s.at[n]))
        loads[n].start()
    low = lax.broadcasted_iota(jnp.int32, (C, KH), 1) < 64
    stores = []
    for kk in range(2):
        for m in range(2):
            rows_of = xm[kk, m].reshape(C, KH)
            swapped = pltpu.roll(rows_of, 64, 1)
            xr[m] = jnp.where(low, rows_of, swapped).reshape(NQ, NI, KH)
            xi[m] = jnp.where(low, swapped, rows_of).reshape(NQ, NI, KH)
            turned[m] = pltpu.roll(gm[kk, m], 64, 1) * -half_sign()
        for i in range(NI):

            def terms(q4, carry):
                for n in range(4):
                    qq = q4 * 4 + n
                    total = jnp.zeros((C, KH), F32)
                    for m in range(2):
                        total = total + xr[m, qq, i : i + 1] * gm[kk, m] + xi[m, qq, i : i + 1] * turned[m]
                    wg[kk, 0, 16 * i + qq] = total[:, :64]
                    wg[kk, 1, 16 * i + qq] = total[:, 64:]
                return carry

            lax.fori_loop(0, NQ // 4, terms, 0)
            for part in range(2):
                block = (kk, part, pl.ds(16 * i, 16))
                stores.append(pltpu.make_async_copy(wg.at[block], wg_hbm.at[block], store_w.at[kk, part, i]))
                stores[-1].start()
            if kk == 0:
                loads[i].wait()
                passes[i].start()
    for store in stores + passes:
        store.wait()


def local(surface, cotangent, spectral_weight, local_weight, bias_vector):
    columns, rows = tables()
    t1 = jnp.asarray(columns, BF)
    t1t = jnp.asarray(columns.T, BF)
    row_table = jnp.asarray(rows, BF)
    gather, spread, natural = (jnp.asarray(p, BF) for p in permutations())
    anywhere = pl.BlockSpec(memory_space=pl.ANY)
    vmem = pl.BlockSpec(memory_space=pltpu.VMEM)
    DMA = pltpu.SemaphoreType.DMA
    V = pltpu.VMEM
    shape = jax.ShapeDtypeStruct
    surface_gradient, xm, gm = pl.pallas_call(
        transfers,
        out_shape=(
            shape((ROWS, W), BF),
            shape((2, 2, NQ, NI, KH), F32),
            shape((2, 2, C, KH), F32),
        ),
        in_specs=[anywhere] * 6 + [vmem] * 5,
        out_specs=[anywhere] * 3,
        scratch_shapes=[
            V((ROWS, W), BF),
            V((ROWS, W), BF),
            V((2, 2, C, C, 64), BF),
            V((W, 2 * KW), BF),
            V((2 * KW, W), BF),
            V((2 * CHUNK, 2 * KH), BF),
            V((2, C, C, KH), F32),
            V((2, C, C, KH), F32),
            V((CHUNK, ROWS), BF),
            V((ROWS, W), F32),
            V((ROWS, W), BF),
            V((2, 2, NI, NQ, R, 2 * KO), BF),
            V((2, 2, NI, NQ, R, 2 * KO), BF),
            V((2, 2, NI, NZ, NQ, 2 * KH), BF),
            V((2, 2, NI, NZ, NQ, 2 * KH), BF),
            V((2, 2, 2, NQ, NI, KH), F32),
            V((2, 2, 2, NQ, NI, KH), F32),
            V((2, 2, 2, NQ, NI, KH), F32),
            V((2, 2, 2, NQ, NI, KH), F32),
            V((2, 2, NI, NQ, 2 * KH), BF),
            V((2, 2, NI, NZ, NQ, 2 * KH), BF),
            V((2, 2, NI, NQ, R, 2 * KO), BF),
            V((2, 2, NI, NQ, R, 2 * KO), BF),
            V((2, NQ, NI, KH), F32),
            V((2, C, KH), F32),
            V((2, 2, C, KH), F32),
            DMA((9,)),
            DMA((NI + 2,)),
            DMA((2, 2, NI)),
            DMA((2, 2, NI)),
            DMA((2, 2, NI)),
            DMA((2, 2)),
            DMA((2, 2, 2)),
            DMA((2, 2)),
            DMA((2, 2, 2)),
            DMA((2, 2)),
            DMA((2, 2, NI)),
            DMA((2, 2, NI)),
            DMA((2, 2, NI)),
            DMA((2, 2, NI)),
        ],
        compiler_params=pltpu.CompilerParams(
            collective_id=0, has_side_effects=True, vmem_limit_bytes=56 * 1024 * 1024
        ),
        name="transfers",
    )(
        surface.reshape(ROWS, W),
        cotangent.reshape(ROWS, W),
        spectral_weight,
        t1,
        t1t,
        row_table,
        local_weight,
        bias_vector.reshape(1, C),
        gather,
        spread,
        natural,
    )
    surface_gradient, weight_gradient = pl.pallas_call(
        outputs,
        out_shape=(shape((ROWS, W), BF), shape((2, 2, C, C, 64), F32)),
        in_specs=[anywhere, vmem, vmem],
        out_specs=[anywhere] * 2,
        scratch_shapes=[
            V((ROWS, W), BF),
            V((2, 2, C, C, 64), F32),
            V((2, NQ, NI, KH), F32),
            V((2, NQ, NI, KH), F32),
            V((2, C, KH), F32),
            DMA((NI,)),
            DMA((NI,)),
            DMA((2, 2, NI)),
        ],
        compiler_params=pltpu.CompilerParams(vmem_limit_bytes=56 * 1024 * 1024),
        name="outputs",
    )(surface_gradient, xm, gm)
    return surface_gradient.reshape(1, C, R, W), weight_gradient


def solution(mesh):
    placed = (
        P("batch", None, "rows", None),
        P("batch", None, "rows", None),
        P("rows", None, None, None, "batch"),
        P(),
        P(),
    )
    return jax.shard_map(
        local,
        mesh=mesh,
        in_specs=placed,
        out_specs=(P("batch", None, "rows", None), P("rows", None, None, None, "batch")),
        check_vma=False,
    )
```

```python
import math

import jax
import jax.numpy as jnp
import numpy as np
from jax import lax
from jax.experimental import pallas as pl
from jax.experimental.pallas import tpu as pltpu
from jax.sharding import PartitionSpec as P

MESH = pl.DeviceIdType.MESH
BF = jnp.bfloat16
F32 = jnp.float32

C = 64
R = 16
W = 1024
KW = 256
KO = KW // 2
KH = 128
NZ = 8
NQ = 16
NI = 4
ROWS = C * R
CHUNK = NQ * R


def tables():
    w = np.arange(W)[:, None]
    columns = []
    for kk in range(2):
        k = 2 * np.arange(KO)[None, :] + kk
        angle = 2 * np.pi * ((w * k) % W) / W
        columns += [np.cos(angle), -np.sin(angle)]
    columns = np.concatenate(columns, axis=1)
    height = NZ * NQ * R
    jj = np.arange(KH // 2)
    rows = np.zeros((NZ, 2 * CHUNK, 2 * KH))
    for z in range(NZ):
        h = (z * CHUNK + np.arange(CHUNK))[:, None]
        for half in range(2):
            f = (jj - half * (KH // 2))[None, :]
            angle = 2 * np.pi * ((f * h) % height) / height
            cos, sin = np.cos(angle), np.sin(angle)
            at = half * KH
            rows[z, :CHUNK, at : at + 64] = cos
            rows[z, :CHUNK, at + 64 : at + 128] = -sin
            rows[z, CHUNK:, at : at + 64] = sin
            rows[z, CHUNK:, at + 64 : at + 128] = cos
    return columns, rows


def permutations():
    gather = np.zeros((NQ, NI, NI, NZ, NQ))
    spread = np.zeros((NQ, NI, C))
    for q in range(NQ):
        for i in range(NI):
            gather[q, i, i, :, q] = 1
            spread[q, i, 16 * i + q] = 1
    gather = gather.reshape(64, 512)
    spread = spread.reshape(64, 64)
    return gather, spread, spread.T.copy()


def dot(a, b, ca=1, cb=0):
    return lax.dot_general(a, b, (((ca,), (cb,)), ((), ())), preferred_element_type=F32)


def gelu_slope(v):
    cumulative = 0.5 * (1.0 + lax.erf(v * (1.0 / math.sqrt(2.0))))
    density = jnp.exp(-0.5 * v * v) * (1.0 / math.sqrt(2.0 * math.pi))
    return cumulative + v * density


def expand_matrix(start):
    row = lax.broadcasted_iota(jnp.int32, (CHUNK, C), 0) + start
    col = lax.broadcasted_iota(jnp.int32, (CHUNK, C), 1)
    return (row // R == col).astype(F32).astype(BF)


def same_row_mask():
    row = lax.broadcasted_iota(jnp.int32, (CHUNK, CHUNK), 0) % R
    col = lax.broadcasted_iota(jnp.int32, (CHUNK, CHUNK), 1) % R
    return row == col


def mix_rows(weight_rows):
    mask = same_row_mask()
    for i in range(NI):
        spread = dot(weight_rows, expand_matrix(i * CHUNK), 1, 1)
        yield i, jnp.where(mask, spread, 0.0).astype(BF)


def column_scale(kk):
    if kk:
        return jnp.full((1, 2 * KO), 2.0**-20, F32)
    lane = lax.broadcasted_iota(jnp.int32, (1, 2 * KO), 1)
    return jnp.where(lane % KO == 0, 2.0**-21, 2.0**-20).astype(F32)


def half_sign():
    lane = lax.broadcasted_iota(jnp.int32, (1, 128), 1)
    return jnp.where(lane < 64, -1.0, 1.0).astype(F32)


def transfers(
    x_hbm, cot_hbm, w_hbm, t1_hbm, t1t_hbm, rows_hbm, lw_hbm, bias_hbm, gather_hbm, spread_hbm, natural_hbm,
    sg_hbm, xm_hbm, gm_hbm,
    lw_ref, bias_ref, gather_ref, spread_ref, natural_ref, x, cot, w, t1, t1t, rt, w2r, w2i, kron, pre, slopes,
    a_out, a_in, b_out, b_in, c_out, c_in, d_out, d_in, e_out, e_in, f_out, f_in, turned, mixed, nat,
    load, store, sa, ra, sb, rb, sc, rc, sd, rd, se, re, sf, rf,
):
    b = lax.axis_index("batch")
    d = lax.axis_index("rows")
    z = d // NQ
    q = d % NQ

    def in_plane(p):
        return lax.rem(q + p, NQ)

    def along(p):
        return lax.rem(z + p, NZ)

    def wait(ref, sem):
        pltpu.make_async_copy(ref, ref, sem).wait()

    def send(src, dst, s, r, batch, row):
        pltpu.make_async_remote_copy(
            src_ref=src, dst_ref=dst, send_sem=s, recv_sem=r, device_id=(batch, row), device_id_type=MESH
        ).start()

    def loop(lo, hi, body):
        def step(p, carry):
            body(p)
            return carry

        lax.fori_loop(lo, hi, step, 0)

    barrier = pltpu.get_barrier_semaphore()

    def greet(batch, row):
        pl.semaphore_signal(barrier, inc=1, device_id=(batch, row), device_id_type=MESH)

    loads = []
    for i in range(NI):
        part = pl.ds(i * CHUNK, CHUNK)
        loads.append(pltpu.make_async_copy(x_hbm.at[part], x.at[part], load.at[i]))
    load_t1 = pltpu.make_async_copy(t1_hbm, t1, load.at[4])
    load_rows = pltpu.make_async_copy(rows_hbm.at[z], rt, load.at[5])
    load_w = pltpu.make_async_copy(w_hbm, w, load.at[6])
    load_t1t = pltpu.make_async_copy(t1t_hbm, t1t, load.at[7])
    load_cot = pltpu.make_async_copy(cot_hbm, cot, load.at[8])
    smalls = []
    for n, (src, dst) in enumerate(
        (
            (lw_hbm, lw_ref),
            (bias_hbm, bias_ref),
            (gather_hbm, gather_ref),
            (spread_hbm, spread_ref),
            (natural_hbm, natural_ref),
        )
    ):
        smalls.append(pltpu.make_async_copy(src, dst, load.at[9 + n]))
    load_t1.start()
    for copy in loads:
        copy.start()
    loop(1, NQ, lambda p: greet(b, z * NQ + in_plane(p)))
    loop(0, NQ, lambda p: greet(1 - b, z * NQ + p))
    loop(1, NZ, lambda p: greet(b, along(p) * NQ + q))
    for copy in (load_rows, load_w, *smalls, load_t1t, load_cot):
        copy.start()

    def split_columns(rnd, i, rows_of):
        field = dot(rows_of, t1[...])
        for kk in range(2):
            half = field[:, kk * 256 : (kk + 1) * 256]
            if rnd:
                half = half * column_scale(kk)
            a_out[rnd, kk, i] = half.astype(BF).reshape(NQ, R, 256)

    load_t1.wait()

    def first(i):
        part = pl.ds(pl.multiple_of(jnp.int32(i) * CHUNK, CHUNK), CHUNK)
        pltpu.make_async_copy(x_hbm.at[part], x.at[part], load.at[i]).wait()
        split_columns(0, i, x[part])

    first(0)
    pl.semaphore_wait(barrier, 2 * NQ - 1 + NZ - 1)

    def send_plane(out, into, s, r, rnd, kk, i):
        def one(p):
            to = in_plane(p)
            send(
                out.at[rnd, kk, i, to], into.at[rnd, kk, i, q], s.at[rnd, kk, i], r.at[rnd, kk, i], b, z * NQ + to
            )

        loop(1, NQ, one)
        pltpu.make_async_copy(out.at[rnd, kk, i, q], into.at[rnd, kk, i, q], r.at[rnd, kk, i]).start()

    def sent_plane(out, s, rnd, kk, i):
        wait(out.at[rnd, kk, i, pl.ds(0, NQ - 1)], s.at[rnd, kk, i])

    def send_owners(out, into, s, r, rnd, kk):
        def same(p):
            to = in_plane(p)
            send(
                out.at[rnd, kk, b, to], into.at[rnd, kk, b, q], s.at[rnd, kk, 0], r.at[rnd, kk], b, z * NQ + to
            )

        def other(p):
            to = in_plane(p)
            send(
                out.at[rnd, kk, 1 - b, to], into.at[rnd, kk, b, q], s.at[rnd, kk, 1], r.at[rnd, kk], 1 - b, z * NQ + to
            )

        loop(0, NQ, other)
        loop(1, NQ, same)
        pltpu.make_async_copy(out.at[rnd, kk, b, q], into.at[rnd, kk, b, q], r.at[rnd, kk]).start()

    def to_modes(rnd, kk):
        def one_channel(i):
            wait(a_in.at[rnd, kk, i], ra.at[rnd, kk, i])
            plane = a_in[rnd, kk, i].reshape(CHUNK, 2 * KO)
            term = dot(plane[:, :KO], rt[:CHUNK], 0, 0) + dot(plane[:, KO:], rt[CHUNK:], 0, 0)
            b_out[rnd, kk, i] = term.astype(BF).reshape(NZ, NQ, 2 * KH)

            def one(p):
                to = along(p)
                send(
                    b_out.at[rnd, kk, i, to], b_in.at[rnd, kk, i, z], sb.at[rnd, kk, i], rb.at[rnd, kk], b, to * NQ + q
                )

            loop(1, NZ, one)
            pltpu.make_async_copy(b_out.at[rnd, kk, i, z], b_in.at[rnd, kk, i, z], rb.at[rnd, kk]).start()

        loop(0, NI, one_channel)

    def to_owners(rnd, kk):
        wait(b_in.at[rnd, kk], rb.at[rnd, kk])
        total = dot(gather_ref[...], b_in[rnd, kk].reshape(512, 2 * KH))
        for half in range(2):
            c_out[rnd, kk, half] = total[:, half * KH : (half + 1) * KH].reshape(NQ, NI, KH)
        send_owners(c_out, c_in, sc, rc, rnd, kk)

    def from_owners(rnd, kk):
        for m in range(2):
            d_out[rnd, kk, m] = dot(spread_ref[...], mixed[m].astype(BF)).reshape(NQ, NI, KH)
        send_owners(d_out, d_in, sd, rd, rnd, kk)

    def narrow_modes(rnd, kk):
        wait(d_in.at[rnd, kk], rd.at[rnd, kk])
        halves = [dot(natural_ref[...], d_in[rnd, kk, half].reshape(C, KH).astype(BF)) for half in range(2)]
        e_out[rnd, kk] = jnp.concatenate(halves, axis=1).astype(BF).reshape(NI, NQ, 2 * KH)

    def spread_modes(rnd, kk, lo=0, hi=NI):
        def one_channel(i):
            def one(p):
                to = along(p)
                send(e_out.at[rnd, kk, i], e_in.at[rnd, kk, i, z], se.at[rnd, kk, i], re.at[rnd, kk, i], b, to * NQ + q)

            loop(1, NZ, one)
            pltpu.make_async_copy(e_out.at[rnd, kk, i], e_in.at[rnd, kk, i, z], re.at[rnd, kk, i]).start()

        loop(lo, hi, one_channel)

    def to_rows(rnd, kk, lo=0, hi=NI):
        def one_channel(i):
            wait(e_in.at[rnd, kk, i], re.at[rnd, kk, i])
            both = dot(rt[...], e_in[rnd, kk, i].reshape(KO, 2 * KH), 1, 1)
            both = jnp.concatenate([both[:CHUNK], both[CHUNK:]], axis=1)
            if rnd == 0:
                both = both * column_scale(kk)
            f_out[rnd, kk, i] = both.astype(BF).reshape(NQ, R, 2 * KO)
            send_plane(f_out, f_in, sf, rf, rnd, kk, i)

        loop(lo, hi, one_channel)

    def row_part(rnd, kk, i):
        wait(f_in.at[rnd, kk, i], rf.at[rnd, kk, i])
        start = pl.multiple_of(i * CHUNK, CHUNK)
        field = dot(f_in[rnd, kk, i].reshape(CHUNK, 2 * KO), t1t[kk * 256 : (kk + 1) * 256])
        return pre[pl.ds(start, CHUNK)] + field

    def add_even(rnd):
        def one_channel(i):
            pre[pl.ds(pl.multiple_of(i * CHUNK, CHUNK), CHUNK)] = row_part(rnd, 0, i)

        loop(0, NI, one_channel)

    def pointwise(rnd, lo, hi):
        field, over = ((x, 1), (slopes, 0))[rnd]

        def rows_of_one(n):
            start = pl.multiple_of(n * CHUNK, CHUNK)
            mine = expand_matrix(start)
            for i, block in mix_rows(dot(mine, lw_ref[...], 1, over).astype(BF)):
                kron[:, i * CHUNK : (i + 1) * CHUNK] = block
            part = pl.ds(start, CHUNK)
            pre[part] = dot(kron[...], field[...])
            if rnd == 0:
                pre[part] += jnp.sum(mine.astype(F32) * bias_ref[...], axis=1, keepdims=True)

        loop(lo, hi, rows_of_one)

    def widen(c):
        for kk in range(2):
            for part, wide in enumerate((w2r, w2i)):
                block = w[kk, part, c].astype(F32)
                wide[kk, c] = jnp.concatenate([block, block], axis=1)

    def mix(kk):
        wait(c_in.at[0, kk], rc.at[0, kk])
        for m in range(2):
            rows_of = c_in[0, kk, m].reshape(C, KH)
            turned[m] = (pltpu.roll(rows_of, 64, 1) * half_sign()).reshape(NQ, NI, KH)

        def terms(qq, sums):
            sums = list(sums)
            for i in range(NI):
                real = w2r[kk, 16 * i + qq]
                imag = w2i[kk, 16 * i + qq]
                for m in range(2):
                    sums[m] = sums[m] + c_in[0, kk, m, qq, i : i + 1] * real + turned[m, qq, i : i + 1] * imag
            return tuple(sums)

        sums = lax.fori_loop(0, NQ, terms, (jnp.zeros((C, KH), F32),) * 2)
        for m in range(2):
            mixed[m] = sums[m]

    def mix_back(kk):
        wait(c_in.at[1, kk], rc.at[1, kk])
        grads = []
        grads_turned = []
        for m in range(2):
            grads.append(dot(natural_ref[...], c_in[1, kk, m].reshape(C, KH).astype(BF)))
            grads_turned.append(pltpu.roll(grads[m], 64, 1) * -half_sign())
            nat[kk, m] = grads[m]

        def terms(c8):
            rows_of = ([], [])
            for n in range(8):
                c = c8 * 8 + n
                real = w2r[kk, c]
                imag = w2i[kk, c]
                for m in range(2):
                    rows_of[m].append(jnp.sum(grads[m] * real + grads_turned[m] * imag, axis=0, keepdims=True))
            for m in range(2):
                mixed[m, pl.ds(pl.multiple_of(c8 * 8, 8), 8)] = jnp.concatenate(rows_of[m], axis=0)

        loop(0, C // 8, terms)

    send_plane(a_out, a_in, sa, ra, 0, 0, 0)

    def first_and_send(i):
        first(i)
        send_plane(a_out, a_in, sa, ra, 0, 0, i)

    loop(1, NI, first_and_send)
    load_w.wait()
    loop(0, 24, widen)
    for copy in smalls:
        copy.wait()
    for i in range(NI):
        sent_plane(a_out, sa, 0, 0, i)
        send_plane(a_out, a_in, sa, ra, 0, 1, i)
        if i < 2:
            pointwise(0, i, i + 1)
    load_rows.wait()
    to_modes(0, 0)
    loop(24, 40, widen)
    to_modes(0, 1)
    to_owners(0, 0)
    loop(40, C, widen)
    mix(0)
    from_owners(0, 0)
    to_owners(0, 1)
    pointwise(0, 2, 4)
    narrow_modes(0, 0)
    spread_modes(0, 0, 0, 2)
    mix(1)
    from_owners(0, 1)
    spread_modes(0, 0, 2, 4)
    to_rows(0, 0, 0, 2)
    narrow_modes(0, 1)
    spread_modes(0, 1)
    to_rows(0, 0, 2, 4)
    to_rows(0, 1)
    copy_xm = pltpu.make_async_copy(c_in.at[0], xm_hbm, store.at[NI])
    copy_xm.start()

    load_t1t.wait()
    add_even(0)
    load_cot.wait()

    def second(i):
        start = pl.multiple_of(i * CHUNK, CHUNK)
        part = pl.ds(start, CHUNK)
        pre[part] = row_part(0, 1, i)

        def slab(s):
            at = pl.ds(pl.multiple_of(start + s * 16, 16), 16)
            slopes[at] = (cot[at].astype(F32) * gelu_slope(pre[at])).astype(BF)

        loop(0, CHUNK // 16, slab)
        split_columns(1, i, slopes[part])
        send_plane(a_out, a_in, sa, ra, 1, 0, i)

    loop(0, NI, second)
    for i in range(NI):
        send_plane(a_out, a_in, sa, ra, 1, 1, i)
    to_modes(1, 0)
    to_modes(1, 1)
    to_owners(1, 0)
    pointwise(1, 0, 4)
    mix_back(0)
    from_owners(1, 0)
    to_owners(1, 1)
    narrow_modes(1, 0)
    spread_modes(1, 0, 0, 2)
    mix_back(1)
    from_owners(1, 1)
    spread_modes(1, 0, 2, 4)
    to_rows(1, 0, 0, 2)
    narrow_modes(1, 1)
    spread_modes(1, 1)
    to_rows(1, 0, 2, 4)
    to_rows(1, 1)
    add_even(1)
    copy_gm = pltpu.make_async_copy(nat, gm_hbm, store.at[NI + 1])
    copy_gm.start()

    def last(i):
        part = pl.ds(pl.multiple_of(i * CHUNK, CHUNK), CHUNK)
        x[part] = row_part(1, 1, i).astype(BF)
        pltpu.make_async_copy(x.at[part], sg_hbm.at[part], store.at[i]).start()

    loop(0, NI, last)

    for i in range(NI):
        part = pl.ds(i * CHUNK, CHUNK)
        pltpu.make_async_copy(x.at[part], sg_hbm.at[part], store.at[i]).wait()
    copy_xm.wait()
    copy_gm.wait()
    for rnd in range(2):
        for kk in range(2):

            def ended(i):
                sent_plane(f_out, sf, rnd, kk, i)
                wait(b_out.at[rnd, kk, i, pl.ds(0, NZ - 1)], sb.at[rnd, kk, i])
                wait(e_in.at[rnd, kk, i, pl.ds(0, NZ - 1)], se.at[rnd, kk, i])
                if rnd or kk:
                    sent_plane(a_out, sa, rnd, kk, i)

            loop(0, NI, ended)
            for out, s in ((c_out, sc), (d_out, sd)):
                wait(out.at[rnd, kk, 0, pl.ds(0, NQ - 1)], s.at[rnd, kk, 0])
                wait(out.at[rnd, kk, 0], s.at[rnd, kk, 1])


def outputs(sg_in, xm_hbm, gm_hbm, sg_hbm, wg_hbm, xm, gm, sg, wg, xr, xi, turned, load, store_s, store_w):
    modes = [pltpu.make_async_copy(xm_hbm, xm, load.at[NI]), pltpu.make_async_copy(gm_hbm, gm, load.at[NI + 1])]
    for copy in modes:
        copy.start()
    loads, passes = [], []
    for n in range(NI):
        part = pl.ds(n * CHUNK, CHUNK)
        loads.append(pltpu.make_async_copy(sg_in.at[part], sg.at[part], load.at[n]))
        passes.append(pltpu.make_async_copy(sg.at[part], sg_hbm.at[part], store_s.at[n]))
        loads[n].start()
    low = lax.broadcasted_iota(jnp.int32, (C, KH), 1) < 64
    stores = []
    for copy in modes:
        copy.wait()
    for kk in range(2):
        for m in range(2):
            rows_of = xm[kk, m].reshape(C, KH)
            swapped = pltpu.roll(rows_of, 64, 1)
            xr[m] = jnp.where(low, rows_of, swapped).reshape(NQ, NI, KH)
            xi[m] = jnp.where(low, swapped, rows_of).reshape(NQ, NI, KH)
            turned[m] = pltpu.roll(gm[kk, m], 64, 1) * -half_sign()
        for i in range(NI):

            def terms(q4, carry):
                for n in range(4):
                    qq = q4 * 4 + n
                    total = jnp.zeros((C, KH), F32)
                    for m in range(2):
                        total = total + xr[m, qq, i : i + 1] * gm[kk, m] + xi[m, qq, i : i + 1] * turned[m]
                    wg[kk, 0, 16 * i + qq] = total[:, :64]
                    wg[kk, 1, 16 * i + qq] = total[:, 64:]
                return carry

            lax.fori_loop(0, NQ // 4, terms, 0)
            for part in range(2):
                block = (kk, part, pl.ds(16 * i, 16))
                stores.append(pltpu.make_async_copy(wg.at[block], wg_hbm.at[block], store_w.at[kk, part, i]))
                stores[-1].start()
            if kk == 0:
                loads[i].wait()
                passes[i].start()
    for store in stores + passes:
        store.wait()


def local(surface, cotangent, spectral_weight, local_weight, bias_vector):
    columns, rows = tables()
    t1 = jnp.asarray(columns, BF)
    t1t = jnp.asarray(columns.T, BF)
    row_table = jnp.asarray(rows, BF)
    gather, spread, natural = (jnp.asarray(p, BF) for p in permutations())
    anywhere = pl.BlockSpec(memory_space=pl.ANY)
    DMA = pltpu.SemaphoreType.DMA
    V = pltpu.VMEM
    shape = jax.ShapeDtypeStruct
    surface_gradient, xm, gm = pl.pallas_call(
        transfers,
        out_shape=(
            shape((ROWS, W), BF),
            shape((2, 2, NQ, NI, KH), F32),
            shape((2, 2, C, KH), F32),
        ),
        in_specs=[anywhere] * 11,
        out_specs=[anywhere] * 3,
        scratch_shapes=[
            V((C, C), BF),
            V((1, C), F32),
            V((64, 512), BF),
            V((64, 64), BF),
            V((64, 64), BF),
            V((ROWS, W), BF),
            V((ROWS, W), BF),
            V((2, 2, C, C, 64), BF),
            V((W, 2 * KW), BF),
            V((2 * KW, W), BF),
            V((2 * CHUNK, 2 * KH), BF),
            V((2, C, C, KH), F32),
            V((2, C, C, KH), F32),
            V((CHUNK, ROWS), BF),
            V((ROWS, W), F32),
            V((ROWS, W), BF),
            V((2, 2, NI, NQ, R, 2 * KO), BF),
            V((2, 2, NI, NQ, R, 2 * KO), BF),
            V((2, 2, NI, NZ, NQ, 2 * KH), BF),
            V((2, 2, NI, NZ, NQ, 2 * KH), BF),
            V((2, 2, 2, NQ, NI, KH), F32),
            V((2, 2, 2, NQ, NI, KH), F32),
            V((2, 2, 2, NQ, NI, KH), F32),
            V((2, 2, 2, NQ, NI, KH), F32),
            V((2, 2, NI, NQ, 2 * KH), BF),
            V((2, 2, NI, NZ, NQ, 2 * KH), BF),
            V((2, 2, NI, NQ, R, 2 * KO), BF),
            V((2, 2, NI, NQ, R, 2 * KO), BF),
            V((2, NQ, NI, KH), F32),
            V((2, C, KH), F32),
            V((2, 2, C, KH), F32),
            DMA((14,)),
            DMA((NI + 2,)),
            DMA((2, 2, NI)),
            DMA((2, 2, NI)),
            DMA((2, 2, NI)),
            DMA((2, 2)),
            DMA((2, 2, 2)),
            DMA((2, 2)),
            DMA((2, 2, 2)),
            DMA((2, 2)),
            DMA((2, 2, NI)),
            DMA((2, 2, NI)),
            DMA((2, 2, NI)),
            DMA((2, 2, NI)),
        ],
        compiler_params=pltpu.CompilerParams(
            collective_id=0, has_side_effects=True, vmem_limit_bytes=56 * 1024 * 1024
        ),
        name="transfers",
    )(
        surface.reshape(ROWS, W),
        cotangent.reshape(ROWS, W),
        spectral_weight,
        t1,
        t1t,
        row_table,
        local_weight,
        bias_vector.reshape(1, C),
        gather,
        spread,
        natural,
    )
    surface_gradient, weight_gradient = pl.pallas_call(
        outputs,
        out_shape=(shape((ROWS, W), BF), shape((2, 2, C, C, 64), F32)),
        in_specs=[anywhere] * 3,
        out_specs=[anywhere] * 2,
        scratch_shapes=[
            V((2, 2, NQ, NI, KH), F32),
            V((2, 2, C, KH), F32),
            V((ROWS, W), BF),
            V((2, 2, C, C, 64), F32),
            V((2, NQ, NI, KH), F32),
            V((2, NQ, NI, KH), F32),
            V((2, C, KH), F32),
            DMA((NI + 2,)),
            DMA((NI,)),
            DMA((2, 2, NI)),
        ],
        compiler_params=pltpu.CompilerParams(vmem_limit_bytes=56 * 1024 * 1024),
        name="outputs",
    )(surface_gradient, xm, gm)
    return surface_gradient.reshape(1, C, R, W), weight_gradient


def solution(mesh):
    placed = (
        P("batch", None, "rows", None),
        P("batch", None, "rows", None),
        P("rows", None, None, None, "batch"),
        P(),
        P(),
    )
    return jax.shard_map(
        local,
        mesh=mesh,
        in_specs=placed,
        out_specs=(P("batch", None, "rows", None), P("rows", None, None, None, "batch")),
        check_vma=False,
    )
```

```python
import math

import jax
import jax.numpy as jnp
import numpy as np
from jax import lax
from jax.experimental import pallas as pl
from jax.experimental.pallas import tpu as pltpu
from jax.sharding import PartitionSpec as P

MESH = pl.DeviceIdType.MESH
BF = jnp.bfloat16
F32 = jnp.float32

C = 64
R = 16
W = 1024
KW = 256
KH = 128
NZ = 8
NQ = 16
NH = 8
NU = 4
NI = 4
ROWS = C * R
CHUNK = NQ * R


def tables():
    w = np.arange(W)[:, None]
    columns = []
    for u in range(NU):
        owner = (NQ * np.arange(NZ)[:, None] + NH * (u % 2) + np.arange(NH)[None, :]).reshape(1, -1)
        k = 2 * owner + u // 2
        angle = 2 * np.pi * ((w * k) % W) / W
        columns += [np.cos(angle), -np.sin(angle)]
    columns = np.concatenate(columns, axis=1)
    height = NZ * NQ * R
    jj = np.arange(KH // 2)
    rows = np.zeros((NZ, CHUNK, 4 * KH))
    for z in range(NZ):
        h = (z * CHUNK + np.arange(CHUNK))[:, None]
        for half in range(2):
            f = (jj - half * (KH // 2))[None, :]
            angle = 2 * np.pi * ((f * h) % height) / height
            cos, sin = np.cos(angle), np.sin(angle)
            at = half * KH
            rows[z, :, at : at + 64] = cos
            rows[z, :, at + 64 : at + 128] = -sin
            rows[z, :, 256 + at : 256 + at + 64] = sin
            rows[z, :, 256 + at + 64 : 256 + at + 128] = cos
    return columns, rows


def permutations():
    gather = np.zeros((NH, NI, 2, NZ, 2, NH))
    spread = np.zeros((NQ, NI, C))
    modes = np.zeros((NI, NH, NH, NI))
    planes = np.zeros((2, NZ, NH, NZ, 2, NH))
    for i in range(NI):
        for q in range(NQ):
            spread[q, i, 16 * i + q] = 1
        for q in range(NH):
            gather[q, i, i // 2, :, i % 2, q] = 1
            modes[i, q, q, i] = 1
            for z in range(NZ):
                planes[i % 2, z, q, z, i % 2, q] = 1
    spread = spread.reshape(64, 64)
    return gather.reshape(32, 256), spread, spread.T.copy(), modes.reshape(32, 32), planes.reshape(128, 128)


def dot(a, b, ca=1, cb=0):
    return lax.dot_general(a, b, (((ca,), (cb,)), ((), ())), preferred_element_type=F32)


def gelu_slope(v):
    cumulative = 0.5 * (1.0 + lax.erf(v * (1.0 / math.sqrt(2.0))))
    density = jnp.exp(-0.5 * v * v) * (1.0 / math.sqrt(2.0 * math.pi))
    return cumulative + v * density


def expand_matrix(start):
    row = lax.broadcasted_iota(jnp.int32, (CHUNK, C), 0) + start
    col = lax.broadcasted_iota(jnp.int32, (CHUNK, C), 1)
    return (row // R == col).astype(F32).astype(BF)


def same_row_mask():
    row = lax.broadcasted_iota(jnp.int32, (CHUNK, CHUNK), 0) % R
    col = lax.broadcasted_iota(jnp.int32, (CHUNK, CHUNK), 1) % R
    return row == col


def mix_rows(weight_rows):
    mask = same_row_mask()
    for i in range(NI):
        spread = dot(weight_rows, expand_matrix(i * CHUNK), 1, 1)
        yield i, jnp.where(mask, spread, 0.0).astype(BF)


def column_scale(u):
    if u:
        return jnp.full((1, 128), 2.0**-20, F32)
    lane = lax.broadcasted_iota(jnp.int32, (1, 128), 1)
    return jnp.where(lane % 64 == 0, 2.0**-21, 2.0**-20).astype(F32)


def half_sign():
    lane = lax.broadcasted_iota(jnp.int32, (1, 128), 1)
    return jnp.where(lane < 64, -1.0, 1.0).astype(F32)


def transfers(
    x_hbm, cot_hbm, w_hbm, t1_hbm, t1t_hbm, rows_hbm, lw_hbm, bias_hbm, gather_hbm, spread_hbm, natural_hbm, modes_hbm,
    planes_hbm,
    sg_hbm, xm_hbm, gm_hbm,
    lw_ref, bias_ref, gather_ref, spread_ref, natural_ref, modes_ref, planes_ref, x, cot, w, t1, t1t, rt, w2r, w2i, kron, pre, slopes,
    a_out, a_in, b_out, b_in, c_out, c_in, d_out, d_in, e_out, e_in, f_out, f_in, turned, mixed, nat,
    load, store, sa, ra, sb, rb, sc, rc, sd, rd, se, re, sf, rf,
):
    b = lax.axis_index("batch")
    d = lax.axis_index("rows")
    z = d // NQ
    q = d % NQ
    qh = q // NH
    q8 = q % NH

    def in_plane(p):
        return lax.rem(q + p, NQ)

    def along(p):
        return lax.rem(z + p, NZ)

    def wait(ref, sem):
        pltpu.make_async_copy(ref, ref, sem).wait()

    def send(src, dst, s, r, batch, row):
        pltpu.make_async_remote_copy(
            src_ref=src, dst_ref=dst, send_sem=s, recv_sem=r, device_id=(batch, row), device_id_type=MESH
        ).start()

    def loop(lo, hi, body):
        def step(p, carry):
            body(p)
            return carry

        lax.fori_loop(lo, hi, step, 0)

    barrier = pltpu.get_barrier_semaphore()

    def greet(batch, row):
        pl.semaphore_signal(barrier, inc=1, device_id=(batch, row), device_id_type=MESH)

    loads = []
    for i in range(NI):
        part = pl.ds(i * CHUNK, CHUNK)
        loads.append(pltpu.make_async_copy(x_hbm.at[part], x.at[part], load.at[i]))
    load_t1 = pltpu.make_async_copy(t1_hbm, t1, load.at[4])
    load_rows = pltpu.make_async_copy(rows_hbm.at[z], rt, load.at[5])
    load_w = pltpu.make_async_copy(w_hbm, w, load.at[6])
    load_t1t = pltpu.make_async_copy(t1t_hbm, t1t, load.at[7])
    load_cot = pltpu.make_async_copy(cot_hbm, cot, load.at[8])
    smalls = []
    for n, (src, dst) in enumerate(
        (
            (lw_hbm, lw_ref),
            (bias_hbm, bias_ref),
            (gather_hbm, gather_ref),
            (spread_hbm, spread_ref),
            (natural_hbm, natural_ref),
            (modes_hbm, modes_ref),
            (planes_hbm, planes_ref),
        )
    ):
        smalls.append(pltpu.make_async_copy(src, dst, load.at[9 + n]))
    load_t1.start()
    for copy in loads:
        copy.start()
    loop(1, NQ, lambda p: greet(b, z * NQ + in_plane(p)))
    loop(0, NQ, lambda p: greet(1 - b, z * NQ + p))
    loop(1, NZ, lambda p: greet(b, along(p) * NQ + q))
    for copy in (load_rows, load_w, *smalls, load_t1t, load_cot):
        copy.start()

    def split_columns(rnd, ip, i2, rows_of, lo=0, hi=NU):
        field = dot(rows_of, t1[:, lo * 128 : hi * 128])
        for u in range(lo, hi):
            part = field[:, (u - lo) * 128 : (u - lo + 1) * 128]
            if rnd:
                part = part * column_scale(u)
            a_out[rnd, u, ip, :, i2] = part.astype(BF).reshape(NQ, R, 128)

    load_t1.wait()

    def first(ip):
        for i2 in range(2):
            part = pl.ds((2 * ip + i2) * CHUNK, CHUNK)
            loads[2 * ip + i2].wait()
            split_columns(0, ip, i2, x[part])

    first(0)
    pl.semaphore_wait(barrier, 2 * NQ - 1 + NZ - 1)

    def send_plane(out, into, s, r, rnd, u, ip):
        def one(p):
            to = in_plane(p)
            send(
                out.at[rnd, u, ip, to], into.at[rnd, u, ip, q], s.at[rnd, u, ip], r.at[rnd, u, ip], b, z * NQ + to
            )

        loop(1, NQ, one)
        pltpu.make_async_copy(out.at[rnd, u, ip, q], into.at[rnd, u, ip, q], r.at[rnd, u, ip]).start()

    def send_channel(rnd, u, ip, i2):
        def one(p):
            to = in_plane(p)
            send(
                a_out.at[rnd, u, ip, to, i2], a_in.at[rnd, u, ip, q, i2], sa.at[rnd, u, ip], ra.at[rnd, u, ip],
                b, z * NQ + to,
            )

        loop(1, NQ, one)
        pltpu.make_async_copy(a_out.at[rnd, u, ip, q, i2], a_in.at[rnd, u, ip, q, i2], ra.at[rnd, u, ip]).start()

    def sent_plane(out, s, rnd, u, ip):
        wait(out.at[rnd, u, ip, pl.ds(0, NQ - 1)], s.at[rnd, u, ip])

    def to_modes(rnd, u, lo=0, hi=2):
        def two_channels(ip):
            wait(a_in.at[rnd, u, ip], ra.at[rnd, u, ip])
            terms = []
            for i2 in range(2):
                both = dot(a_in[rnd, u, ip, :, i2].reshape(CHUNK, 128), rt[...], 0, 0)
                term = both[:64, : 2 * KH] + both[64:, 2 * KH :]
                terms.append(term.reshape(NZ, NH, 2 * KH))
            b_out[rnd, u, ip] = jnp.concatenate(terms, axis=1).astype(BF)

            def one(p):
                to = along(p)
                send(
                    b_out.at[rnd, u, ip, to], b_in.at[rnd, u, ip, z], sb.at[rnd, u, ip], rb.at[rnd, u], b, to * NQ + q
                )

            loop(1, NZ, one)
            pltpu.make_async_copy(b_out.at[rnd, u, ip, z], b_in.at[rnd, u, ip, z], rb.at[rnd, u]).start()

        loop(lo, hi, two_channels)

    def to_owners(rnd, u):
        kk, h = u // 2, u % 2
        wait(b_in.at[rnd, u], rb.at[rnd, u])
        total = dot(gather_ref[...], b_in[rnd, u].reshape(256, 2 * KH))
        for half in range(2):
            c_out[rnd, u, half] = total[:, half * KH : (half + 1) * KH].reshape(NH, NI, KH)

        def other(p):
            to = lax.rem(q8 + p, NH)
            row = z * NQ + h * NH + to
            send(c_out.at[rnd, u, 1 - b, to], c_in.at[rnd, kk, b, q], sc.at[rnd, u, 1], rc.at[rnd, kk], 1 - b, row)

        def same(p):
            to = lax.rem(q8 + p, NH)
            row = z * NQ + h * NH + to
            send(c_out.at[rnd, u, b, to], c_in.at[rnd, kk, b, q], sc.at[rnd, u, 0], rc.at[rnd, kk], b, row)

        loop(0, NH, other)
        loop(1, NH, same)

        @pl.when(qh != h)
        def _():
            same(0)

        @pl.when(qh == h)
        def _():
            pltpu.make_async_copy(c_out.at[rnd, u, b, q8], c_in.at[rnd, kk, b, q], rc.at[rnd, kk]).start()

    def at_owners(rnd, u):
        @pl.when(qh == u % 2)
        def _():
            (mix, mix_back)[rnd](u // 2)
            from_owners(rnd, u)

    def from_owners(rnd, u):
        kk = u // 2
        for m in range(2):
            d_out[rnd, kk, m] = dot(spread_ref[...], mixed[m].astype(BF)).reshape(NQ, NI, KH)

        def other(p):
            to = in_plane(p)
            row = z * NQ + to
            send(d_out.at[rnd, kk, 1 - b, to], d_in.at[rnd, u, b, q8], sd.at[rnd, kk, 1], rd.at[rnd, u], 1 - b, row)

        def same(p):
            to = in_plane(p)
            row = z * NQ + to
            send(d_out.at[rnd, kk, b, to], d_in.at[rnd, u, b, q8], sd.at[rnd, kk, 0], rd.at[rnd, u], b, row)

        loop(0, NQ, other)
        loop(1, NQ, same)
        pltpu.make_async_copy(d_out.at[rnd, kk, b, q], d_in.at[rnd, u, b, q8], rd.at[rnd, u]).start()

    def spread_modes(rnd, u):
        wait(d_in.at[rnd, u], rd.at[rnd, u])
        halves = [dot(modes_ref[...], d_in[rnd, u, half].reshape(32, KH).astype(BF)) for half in range(2)]
        e_out[rnd, u] = jnp.concatenate(halves, axis=1).astype(BF).reshape(2, 2 * NH, 2 * KH)
        for op in range(2):

            def one(p):
                to = along(p)
                send(e_out.at[rnd, u, op], e_in.at[rnd, u, op, z], se.at[rnd, u, op], re.at[rnd, u, op], b, to * NQ + q)

            loop(1, NZ, one)
            pltpu.make_async_copy(e_out.at[rnd, u, op], e_in.at[rnd, u, op, z], re.at[rnd, u, op]).start()

    def to_rows(rnd, u):
        def two_channels(op):
            wait(e_in.at[rnd, u, op], re.at[rnd, u, op])
            spectra = dot(planes_ref[...], e_in[rnd, u, op].reshape(128, 2 * KH)).astype(BF)
            real = dot(rt[:, : 2 * KH], spectra, 1, 1)
            imag = dot(rt[:, 2 * KH :], spectra, 1, 1)
            for o2 in range(2):
                at = slice(64 * o2, 64 * o2 + 64)
                both = jnp.concatenate([real[:, at], imag[:, at]], axis=1)
                if rnd == 0:
                    both = both * column_scale(u)
                f_out[rnd, u, op, :, o2] = both.astype(BF).reshape(NQ, R, 128)
            send_plane(f_out, f_in, sf, rf, rnd, u, op)

        loop(0, 2, two_channels)

    def row_parts(rnd, kk, op):
        us = (2 * kk, 2 * kk + 1)
        for u in us:
            wait(f_in.at[rnd, u, op], rf.at[rnd, u, op])
        for o2 in range(2):
            start = pl.multiple_of((2 * op + o2) * CHUNK, CHUNK)
            part = pl.ds(start, CHUNK)
            rows_of = jnp.concatenate([f_in[rnd, u, op, :, o2].reshape(CHUNK, 128) for u in us], axis=1)
            yield start, part, pre[part] + dot(rows_of, t1t[kk * 256 : (kk + 1) * 256])

    def add_even(rnd):
        def two_channels(op):
            for _, part, total in row_parts(rnd, 0, op):
                pre[part] = total

        loop(0, 2, two_channels)

    def pointwise(rnd, lo, hi):
        field, over = ((x, 1), (slopes, 0))[rnd]

        def rows_of_one(n):
            start = pl.multiple_of(n * CHUNK, CHUNK)
            mine = expand_matrix(start)
            for i, block in mix_rows(dot(mine, lw_ref[...], 1, over).astype(BF)):
                kron[:, i * CHUNK : (i + 1) * CHUNK] = block
            part = pl.ds(start, CHUNK)
            pre[part] = dot(kron[...], field[...])
            if rnd == 0:
                pre[part] += jnp.sum(mine.astype(F32) * bias_ref[...], axis=1, keepdims=True)

        loop(lo, hi, rows_of_one)

    def widen(c):
        for kk in range(2):
            for part, wide in enumerate((w2r, w2i)):
                block = w[kk, part, c].astype(F32)
                wide[kk, c] = jnp.concatenate([block, block], axis=1)

    def mix(kk):
        wait(c_in.at[0, kk], rc.at[0, kk])
        for m in range(2):
            rows_of = c_in[0, kk, m].reshape(C, KH)
            turned[m] = (pltpu.roll(rows_of, 64, 1) * half_sign()).reshape(NQ, NI, KH)

        def terms(qq, sums):
            sums = list(sums)
            for i in range(NI):
                real = w2r[kk, 16 * i + qq]
                imag = w2i[kk, 16 * i + qq]
                for m in range(2):
                    sums[m] = sums[m] + c_in[0, kk, m, qq, i : i + 1] * real + turned[m, qq, i : i + 1] * imag
            return tuple(sums)

        sums = lax.fori_loop(0, NQ, terms, (jnp.zeros((C, KH), F32),) * 2)
        for m in range(2):
            mixed[m] = sums[m]

    def mix_back(kk):
        wait(c_in.at[1, kk], rc.at[1, kk])
        grads = []
        grads_turned = []
        for m in range(2):
            grads.append(dot(natural_ref[...], c_in[1, kk, m].reshape(C, KH).astype(BF)))
            grads_turned.append(pltpu.roll(grads[m], 64, 1) * -half_sign())
            nat[kk, m] = grads[m]

        def terms(c8):
            rows_of = ([], [])
            for n in range(8):
                c = c8 * 8 + n
                real = w2r[kk, c]
                imag = w2i[kk, c]
                for m in range(2):
                    rows_of[m].append(jnp.sum(grads[m] * real + grads_turned[m] * imag, axis=0, keepdims=True))
            for m in range(2):
                mixed[m, pl.ds(pl.multiple_of(c8 * 8, 8), 8)] = jnp.concatenate(rows_of[m], axis=0)

        loop(0, C // 8, terms)

    def transforms(rnd, last_modes, spares):
        to_owners(rnd, 0)
        last_modes(2)
        if rnd == 0:
            loop(48, C, widen)
        to_owners(rnd, 1)
        last_modes(3)
        spares(0)
        at_owners(rnd, 0)
        to_owners(rnd, 2)
        spares(1)
        at_owners(rnd, 1)
        to_owners(rnd, 3)
        spread_modes(rnd, 0)
        at_owners(rnd, 2)
        spread_modes(rnd, 1)
        at_owners(rnd, 3)
        to_rows(rnd, 0)
        spread_modes(rnd, 2)
        to_rows(rnd, 1)
        spread_modes(rnd, 3)
        to_rows(rnd, 2)
        to_rows(rnd, 3)
        spares(2)
        spares(3)
        add_even(rnd)

    def next_piece(rnd, n):
        sent_plane(a_out, sa, rnd, (n - 2) // 2, n % 2)
        send_plane(a_out, a_in, sa, ra, rnd, n // 2, n % 2)

    send_plane(a_out, a_in, sa, ra, 0, 0, 0)
    first(1)
    send_plane(a_out, a_in, sa, ra, 0, 0, 1)
    load_w.wait()
    for copy in smalls:
        copy.wait()
    loop(0, 16, widen)
    next_piece(0, 2)
    loop(16, 32, widen)
    next_piece(0, 3)
    load_rows.wait()
    to_modes(0, 0, 0, 1)
    next_piece(0, 4)
    to_modes(0, 0, 1, 2)
    next_piece(0, 5)
    loop(32, 48, widen)
    to_modes(0, 1, 0, 1)
    next_piece(0, 6)
    to_modes(0, 1, 1, 2)
    next_piece(0, 7)
    load_t1t.wait()
    transforms(0, lambda u: to_modes(0, u), lambda n: pointwise(0, n, n + 1))
    copy_xm = pltpu.make_async_copy(c_in.at[0], xm_hbm, store.at[NI])
    copy_xm.start()

    load_cot.wait()

    def second(op):
        for o2, (start, part, total) in enumerate(row_parts(0, 1, op)):
            pre[part] = total

            def slab(s):
                at = pl.ds(pl.multiple_of(start + s * 16, 16), 16)
                slopes[at] = (cot[at].astype(F32) * gelu_slope(pre[at])).astype(BF)

            loop(0, CHUNK // 16, slab)
            split_columns(1, op, o2, slopes[part], 0, 1)
            send_channel(1, 0, op, o2)

    def other_quarters(op):
        for o2 in range(2):
            start = pl.multiple_of((2 * op + o2) * CHUNK, CHUNK)
            split_columns(1, op, o2, slopes[pl.ds(start, CHUNK)], 1, NU)
        send_plane(a_out, a_in, sa, ra, 1, 1, op)

    loop(0, 2, second)
    loop(0, 2, other_quarters)
    to_modes(1, 0, 0, 1)
    next_piece(1, 4)
    to_modes(1, 0, 1, 2)
    next_piece(1, 5)
    to_modes(1, 1, 0, 1)
    next_piece(1, 6)
    to_modes(1, 1, 1, 2)
    next_piece(1, 7)
    transforms(1, lambda u: to_modes(1, u), lambda n: pointwise(1, n, n + 1))
    copy_gm = pltpu.make_async_copy(nat, gm_hbm, store.at[NI + 1])
    copy_gm.start()

    def last(op):
        for o2, (_, part, total) in enumerate(row_parts(1, 1, op)):
            x[part] = total.astype(BF)
            pltpu.make_async_copy(x.at[part], sg_hbm.at[part], store.at[2 * op + o2]).start()

    loop(0, 2, last)

    for i in range(NI):
        part = pl.ds(i * CHUNK, CHUNK)
        pltpu.make_async_copy(x.at[part], sg_hbm.at[part], store.at[i]).wait()
    copy_xm.wait()
    copy_gm.wait()
    for rnd in range(2):
        for u in range(NU):
            for ip in range(2):
                sent_plane(f_out, sf, rnd, u, ip)
                wait(b_out.at[rnd, u, ip, pl.ds(0, NZ - 1)], sb.at[rnd, u, ip])
                wait(e_in.at[rnd, u, ip, pl.ds(0, NZ - 1)], se.at[rnd, u, ip])
                if u == NU - 1 or (rnd == 1 and u == 0):
                    sent_plane(a_out, sa, rnd, u, ip)
            wait(c_out.at[rnd, u, 0], sc.at[rnd, u, 1])

            @pl.when(qh != u % 2)
            def _():
                wait(c_out.at[rnd, u, 0], sc.at[rnd, u, 0])

            @pl.when(qh == u % 2)
            def _():
                wait(c_out.at[rnd, u, 0, pl.ds(0, NH - 1)], sc.at[rnd, u, 0])

        for kk in range(2):
            wait(d_out.at[rnd, kk, 0, pl.ds(0, NQ - 1)], sd.at[rnd, kk, 0])
            wait(d_out.at[rnd, kk, 0], sd.at[rnd, kk, 1])


def outputs(sg_in, xm_hbm, gm_hbm, sg_hbm, wg_hbm, xm, gm, sg, wg, xr, xi, turned, load, store_s, store_w):
    modes = [pltpu.make_async_copy(xm_hbm, xm, load.at[NI]), pltpu.make_async_copy(gm_hbm, gm, load.at[NI + 1])]
    for copy in modes:
        copy.start()
    loads, passes = [], []
    for n in range(NI):
        part = pl.ds(n * CHUNK, CHUNK)
        loads.append(pltpu.make_async_copy(sg_in.at[part], sg.at[part], load.at[n]))
        passes.append(pltpu.make_async_copy(sg.at[part], sg_hbm.at[part], store_s.at[n]))
        loads[n].start()
    low = lax.broadcasted_iota(jnp.int32, (C, KH), 1) < 64
    stores = []
    for copy in modes:
        copy.wait()
    for kk in range(2):
        for m in range(2):
            rows_of = xm[kk, m].reshape(C, KH)
            swapped = pltpu.roll(rows_of, 64, 1)
            xr[m] = jnp.where(low, rows_of, swapped).reshape(NQ, NI, KH)
            xi[m] = jnp.where(low, swapped, rows_of).reshape(NQ, NI, KH)
            turned[m] = pltpu.roll(gm[kk, m], 64, 1) * -half_sign()
        for i in range(NI):

            def terms(q4, carry):
                for n in range(4):
                    qq = q4 * 4 + n
                    total = jnp.zeros((C, KH), F32)
                    for m in range(2):
                        total = total + xr[m, qq, i : i + 1] * gm[kk, m] + xi[m, qq, i : i + 1] * turned[m]
                    wg[kk, 0, 16 * i + qq] = total[:, :64]
                    wg[kk, 1, 16 * i + qq] = total[:, 64:]
                return carry

            lax.fori_loop(0, NQ // 4, terms, 0)
            for part in range(2):
                block = (kk, part, pl.ds(16 * i, 16))
                stores.append(pltpu.make_async_copy(wg.at[block], wg_hbm.at[block], store_w.at[kk, part, i]))
                stores[-1].start()
            if kk == 0:
                loads[i].wait()
                passes[i].start()
    for store in stores + passes:
        store.wait()


def local(surface, cotangent, spectral_weight, local_weight, bias_vector):
    columns, rows = tables()
    t1 = jnp.asarray(columns, BF)
    t1t = jnp.asarray(columns.T, BF)
    row_table = jnp.asarray(rows, BF)
    gather, spread, natural, modes, planes = (jnp.asarray(p, BF) for p in permutations())
    anywhere = pl.BlockSpec(memory_space=pl.ANY)
    DMA = pltpu.SemaphoreType.DMA
    V = pltpu.VMEM
    shape = jax.ShapeDtypeStruct
    surface_gradient, xm, gm = pl.pallas_call(
        transfers,
        out_shape=(
            shape((ROWS, W), BF),
            shape((2, 2, NQ, NI, KH), F32),
            shape((2, 2, C, KH), F32),
        ),
        in_specs=[anywhere] * 13,
        out_specs=[anywhere] * 3,
        scratch_shapes=[
            V((C, C), BF),
            V((1, C), F32),
            V((32, 256), BF),
            V((64, 64), BF),
            V((64, 64), BF),
            V((32, 32), BF),
            V((128, 128), BF),
            V((ROWS, W), BF),
            V((ROWS, W), BF),
            V((2, 2, C, C, 64), BF),
            V((W, 2 * KW), BF),
            V((2 * KW, W), BF),
            V((CHUNK, 4 * KH), BF),
            V((2, C, C, KH), F32),
            V((2, C, C, KH), F32),
            V((CHUNK, ROWS), BF),
            V((ROWS, W), F32),
            V((ROWS, W), BF),
            V((2, NU, 2, NQ, 2, R, 128), BF),
            V((2, NU, 2, NQ, 2, R, 128), BF),
            V((2, NU, 2, NZ, 2 * NH, 2 * KH), BF),
            V((2, NU, 2, NZ, 2 * NH, 2 * KH), BF),
            V((2, NU, 2, NH, NI, KH), F32),
            V((2, 2, 2, NQ, NI, KH), F32),
            V((2, 2, 2, NQ, NI, KH), F32),
            V((2, NU, 2, NH, NI, KH), F32),
            V((2, NU, 2, 2 * NH, 2 * KH), BF),
            V((2, NU, 2, NZ, 2 * NH, 2 * KH), BF),
            V((2, NU, 2, NQ, 2, R, 128), BF),
            V((2, NU, 2, NQ, 2, R, 128), BF),
            V((2, NQ, NI, KH), F32),
            V((2, C, KH), F32),
            V((2, 2, C, KH), F32),
            DMA((16,)),
            DMA((NI + 2,)),
            DMA((2, NU, 2)),
            DMA((2, NU, 2)),
            DMA((2, NU, 2)),
            DMA((2, NU)),
            DMA((2, NU, 2)),
            DMA((2, 2)),
            DMA((2, 2, 2)),
            DMA((2, NU)),
            DMA((2, NU, 2)),
            DMA((2, NU, 2)),
            DMA((2, NU, 2)),
            DMA((2, NU, 2)),
        ],
        compiler_params=pltpu.CompilerParams(
            collective_id=0, has_side_effects=True, vmem_limit_bytes=56 * 1024 * 1024
        ),
        name="transfers",
    )(
        surface.reshape(ROWS, W),
        cotangent.reshape(ROWS, W),
        spectral_weight,
        t1,
        t1t,
        row_table,
        local_weight,
        bias_vector.reshape(1, C),
        gather,
        spread,
        natural,
        modes,
        planes,
    )
    surface_gradient, weight_gradient = pl.pallas_call(
        outputs,
        out_shape=(shape((ROWS, W), BF), shape((2, 2, C, C, 64), F32)),
        in_specs=[anywhere] * 3,
        out_specs=[anywhere] * 2,
        scratch_shapes=[
            V((2, 2, NQ, NI, KH), F32),
            V((2, 2, C, KH), F32),
            V((ROWS, W), BF),
            V((2, 2, C, C, 64), F32),
            V((2, NQ, NI, KH), F32),
            V((2, NQ, NI, KH), F32),
            V((2, C, KH), F32),
            DMA((NI + 2,)),
            DMA((NI,)),
            DMA((2, 2, NI)),
        ],
        compiler_params=pltpu.CompilerParams(vmem_limit_bytes=56 * 1024 * 1024),
        name="outputs",
    )(surface_gradient, xm, gm)
    return surface_gradient.reshape(1, C, R, W), weight_gradient


def solution(mesh):
    placed = (
        P("batch", None, "rows", None),
        P("batch", None, "rows", None),
        P("rows", None, None, None, "batch"),
        P(),
        P(),
    )
    return jax.shard_map(
        local,
        mesh=mesh,
        in_specs=placed,
        out_specs=(P("batch", None, "rows", None), P("rows", None, None, None, "batch")),
        check_vma=False,
    )
```

```python
import math

import jax
import jax.numpy as jnp
import numpy as np
from jax import lax
from jax.experimental import pallas as pl
from jax.experimental.pallas import tpu as pltpu
from jax.sharding import PartitionSpec as P

MESH = pl.DeviceIdType.MESH
BF = jnp.bfloat16
F32 = jnp.float32

C = 64
R = 16
W = 1024
KW = 256
KH = 128
NZ = 8
NQ = 16
NH = 8
NU = 4
NI = 4
ROWS = C * R
CHUNK = NQ * R


def tables():
    w = np.arange(W)[:, None]
    columns = []
    for u in range(NU):
        owner = (NQ * np.arange(NZ)[:, None] + NH * (u % 2) + np.arange(NH)[None, :]).reshape(1, -1)
        k = 2 * owner + u // 2
        angle = 2 * np.pi * ((w * k) % W) / W
        columns += [np.cos(angle), -np.sin(angle)]
    columns = np.concatenate(columns, axis=1)
    height = NZ * NQ * R
    jj = np.arange(KH // 2)
    rows = np.zeros((NZ, CHUNK, 4 * KH))
    for z in range(NZ):
        h = (z * CHUNK + np.arange(CHUNK))[:, None]
        for half in range(2):
            f = (jj - half * (KH // 2))[None, :]
            angle = 2 * np.pi * ((f * h) % height) / height
            cos, sin = np.cos(angle), np.sin(angle)
            at = half * KH
            rows[z, :, at : at + 64] = cos
            rows[z, :, at + 64 : at + 128] = -sin
            rows[z, :, 256 + at : 256 + at + 64] = sin
            rows[z, :, 256 + at + 64 : 256 + at + 128] = cos
    return columns, rows


def permutations():
    gather = np.zeros((NH, NI, 2, NZ, 2, NH))
    spread = np.zeros((NQ, NI, C))
    modes = np.zeros((NI, NH, NH, NI))
    planes = np.zeros((2, NZ, NH, NZ, 2, NH))
    for i in range(NI):
        for q in range(NQ):
            spread[q, i, 16 * i + q] = 1
        for q in range(NH):
            gather[q, i, i // 2, :, i % 2, q] = 1
            modes[i, q, q, i] = 1
            for z in range(NZ):
                planes[i % 2, z, q, z, i % 2, q] = 1
    spread = spread.reshape(64, 64)
    return gather.reshape(32, 256), spread, spread.T.copy(), modes.reshape(32, 32), planes.reshape(128, 128)


def dot(a, b, ca=1, cb=0):
    return lax.dot_general(a, b, (((ca,), (cb,)), ((), ())), preferred_element_type=F32)


def gelu_slope(v):
    cumulative = 0.5 * (1.0 + lax.erf(v * (1.0 / math.sqrt(2.0))))
    density = jnp.exp(-0.5 * v * v) * (1.0 / math.sqrt(2.0 * math.pi))
    return cumulative + v * density


def expand_matrix(start):
    row = lax.broadcasted_iota(jnp.int32, (CHUNK, C), 0) + start
    col = lax.broadcasted_iota(jnp.int32, (CHUNK, C), 1)
    return (row // R == col).astype(F32).astype(BF)


def same_row_mask():
    row = lax.broadcasted_iota(jnp.int32, (CHUNK, CHUNK), 0) % R
    col = lax.broadcasted_iota(jnp.int32, (CHUNK, CHUNK), 1) % R
    return row == col


def mix_rows(weight_rows):
    mask = same_row_mask()
    for i in range(NI):
        spread = dot(weight_rows, expand_matrix(i * CHUNK), 1, 1)
        yield i, jnp.where(mask, spread, 0.0).astype(BF)


def column_scale(u):
    if u:
        return jnp.full((1, 128), 2.0**-20, F32)
    lane = lax.broadcasted_iota(jnp.int32, (1, 128), 1)
    return jnp.where(lane % 64 == 0, 2.0**-21, 2.0**-20).astype(F32)


def half_sign():
    lane = lax.broadcasted_iota(jnp.int32, (1, 128), 1)
    return jnp.where(lane < 64, -1.0, 1.0).astype(F32)


def transfers(
    x_hbm, cot_hbm, w_hbm, t1_hbm, t1t_hbm, rows_hbm, lw_hbm, bias_hbm, gather_hbm, spread_hbm, natural_hbm, modes_hbm,
    planes_hbm,
    sg_hbm, xm_hbm, gm_hbm,
    lw_ref, bias_ref, gather_ref, spread_ref, natural_ref, modes_ref, planes_ref, x, cot, w, t1, t1t, rt, w2r, w2i, kron, pre, slopes,
    a_out, a_in, b_out, b_in, c_out, c_in, d_out, d_in, e_out, e_in, f_out, f_in, turned, mixed, nat,
    load, store, sa, ra, sb, rb, sc, rc, sd, rd, se, re, sf, rf,
):
    b = lax.axis_index("batch")
    d = lax.axis_index("rows")
    z = d // NQ
    q = d % NQ
    qh = q // NH
    q8 = q % NH

    def in_plane(p):
        return lax.rem(q + p, NQ)

    def along(p):
        return lax.rem(z + p, NZ)

    def wait(ref, sem):
        pltpu.make_async_copy(ref, ref, sem).wait()

    def send(src, dst, s, r, batch, row):
        pltpu.make_async_remote_copy(
            src_ref=src, dst_ref=dst, send_sem=s, recv_sem=r, device_id=(batch, row), device_id_type=MESH
        ).start()

    def loop(lo, hi, body):
        def step(p, carry):
            body(p)
            return carry

        lax.fori_loop(lo, hi, step, 0)

    barrier = pltpu.get_barrier_semaphore()

    def greet(batch, row):
        pl.semaphore_signal(barrier, inc=1, device_id=(batch, row), device_id_type=MESH)

    loads = []
    for i in range(NI):
        part = pl.ds(i * CHUNK, CHUNK)
        loads.append(pltpu.make_async_copy(x_hbm.at[part], x.at[part], load.at[i]))
    load_t1 = pltpu.make_async_copy(t1_hbm, t1, load.at[4])
    load_rows = pltpu.make_async_copy(rows_hbm.at[z], rt, load.at[5])
    load_w = pltpu.make_async_copy(w_hbm, w, load.at[6])
    load_t1t = pltpu.make_async_copy(t1t_hbm, t1t, load.at[7])
    load_cot = pltpu.make_async_copy(cot_hbm, cot, load.at[8])
    smalls = []
    for n, (src, dst) in enumerate(
        (
            (lw_hbm, lw_ref),
            (bias_hbm, bias_ref),
            (gather_hbm, gather_ref),
            (spread_hbm, spread_ref),
            (natural_hbm, natural_ref),
            (modes_hbm, modes_ref),
            (planes_hbm, planes_ref),
        )
    ):
        smalls.append(pltpu.make_async_copy(src, dst, load.at[9 + n]))
    load_t1.start()
    for copy in loads:
        copy.start()
    loop(1, NQ, lambda p: greet(b, z * NQ + in_plane(p)))
    loop(0, NQ, lambda p: greet(1 - b, z * NQ + p))
    loop(1, NZ, lambda p: greet(b, along(p) * NQ + q))
    for copy in (load_rows, load_w, *smalls, load_t1t, load_cot):
        copy.start()

    def split_columns(rnd, ip, i2, rows_of, lo=0, hi=NU):
        field = dot(rows_of, t1[:, lo * 128 : hi * 128])
        for u in range(lo, hi):
            part = field[:, (u - lo) * 128 : (u - lo + 1) * 128]
            if rnd:
                part = part * column_scale(u)
            a_out[rnd, u, ip, :, i2] = part.astype(BF).reshape(NQ, R, 128)

    load_t1.wait()

    for i in range(NI):
        loads[i].wait()
        split_columns(0, i // 2, i % 2, x[i * CHUNK : (i + 1) * CHUNK], 0, 1)
    pl.semaphore_wait(barrier, 2 * NQ - 1 + NZ - 1)

    def send_plane(out, into, s, r, rnd, u, ip):
        def one(p):
            to = in_plane(p)
            send(
                out.at[rnd, u, ip, to], into.at[rnd, u, ip, q], s.at[rnd, u, ip], r.at[rnd, u, ip], b, z * NQ + to
            )

        loop(1, NQ, one)
        pltpu.make_async_copy(out.at[rnd, u, ip, q], into.at[rnd, u, ip, q], r.at[rnd, u, ip]).start()

    def send_channel(rnd, u, ip, i2):
        def one(p):
            to = in_plane(p)
            send(
                a_out.at[rnd, u, ip, to, i2], a_in.at[rnd, u, ip, q, i2], sa.at[rnd, u, ip], ra.at[rnd, u, ip],
                b, z * NQ + to,
            )

        loop(1, NQ, one)
        pltpu.make_async_copy(a_out.at[rnd, u, ip, q, i2], a_in.at[rnd, u, ip, q, i2], ra.at[rnd, u, ip]).start()

    def sent_plane(out, s, rnd, u, ip):
        wait(out.at[rnd, u, ip, pl.ds(0, NQ - 1)], s.at[rnd, u, ip])

    def to_modes(rnd, u, lo=0, hi=2):
        def two_channels(ip):
            wait(a_in.at[rnd, u, ip], ra.at[rnd, u, ip])
            terms = []
            for i2 in range(2):
                both = dot(a_in[rnd, u, ip, :, i2].reshape(CHUNK, 128), rt[...], 0, 0)
                term = both[:64, : 2 * KH] + both[64:, 2 * KH :]
                terms.append(term.reshape(NZ, NH, 2 * KH))
            b_out[rnd, u, ip] = jnp.concatenate(terms, axis=1).astype(BF)

            def one(p):
                to = along(p)
                send(
                    b_out.at[rnd, u, ip, to], b_in.at[rnd, u, ip, z], sb.at[rnd, u, ip], rb.at[rnd, u], b, to * NQ + q
                )

            loop(1, NZ, one)
            pltpu.make_async_copy(b_out.at[rnd, u, ip, z], b_in.at[rnd, u, ip, z], rb.at[rnd, u]).start()

        loop(lo, hi, two_channels)

    def to_owners(rnd, u):
        kk, h = u // 2, u % 2
        wait(b_in.at[rnd, u], rb.at[rnd, u])
        total = dot(gather_ref[...], b_in[rnd, u].reshape(256, 2 * KH))
        for half in range(2):
            c_out[rnd, u, half] = total[:, half * KH : (half + 1) * KH].reshape(NH, NI, KH)

        def other(p):
            to = lax.rem(q8 + p, NH)
            row = z * NQ + h * NH + to
            send(c_out.at[rnd, u, 1 - b, to], c_in.at[rnd, kk, b, q], sc.at[rnd, u, 1], rc.at[rnd, kk], 1 - b, row)

        def same(p):
            to = lax.rem(q8 + p, NH)
            row = z * NQ + h * NH + to
            send(c_out.at[rnd, u, b, to], c_in.at[rnd, kk, b, q], sc.at[rnd, u, 0], rc.at[rnd, kk], b, row)

        loop(0, NH, other)
        loop(1, NH, same)

        @pl.when(qh != h)
        def _():
            same(0)

        @pl.when(qh == h)
        def _():
            pltpu.make_async_copy(c_out.at[rnd, u, b, q8], c_in.at[rnd, kk, b, q], rc.at[rnd, kk]).start()

    def at_owners(rnd, u):
        @pl.when(qh == u % 2)
        def _():
            (mix, mix_back)[rnd](u // 2)
            from_owners(rnd, u)

    def from_owners(rnd, u):
        kk = u // 2
        for m in range(2):
            d_out[rnd, kk, m] = dot(spread_ref[...], mixed[m].astype(BF)).reshape(NQ, NI, KH)

        def other(p):
            to = in_plane(p)
            row = z * NQ + to
            send(d_out.at[rnd, kk, 1 - b, to], d_in.at[rnd, u, b, q8], sd.at[rnd, kk, 1], rd.at[rnd, u], 1 - b, row)

        def same(p):
            to = in_plane(p)
            row = z * NQ + to
            send(d_out.at[rnd, kk, b, to], d_in.at[rnd, u, b, q8], sd.at[rnd, kk, 0], rd.at[rnd, u], b, row)

        loop(0, NQ, other)
        loop(1, NQ, same)
        pltpu.make_async_copy(d_out.at[rnd, kk, b, q], d_in.at[rnd, u, b, q8], rd.at[rnd, u]).start()

    def spread_modes(rnd, u):
        wait(d_in.at[rnd, u], rd.at[rnd, u])
        halves = [dot(modes_ref[...], d_in[rnd, u, half].reshape(32, KH).astype(BF)) for half in range(2)]
        e_out[rnd, u] = jnp.concatenate(halves, axis=1).astype(BF).reshape(2, 2 * NH, 2 * KH)
        for op in range(2):

            def one(p):
                to = along(p)
                send(e_out.at[rnd, u, op], e_in.at[rnd, u, op, z], se.at[rnd, u, op], re.at[rnd, u, op], b, to * NQ + q)

            loop(1, NZ, one)
            pltpu.make_async_copy(e_out.at[rnd, u, op], e_in.at[rnd, u, op, z], re.at[rnd, u, op]).start()

    def to_rows(rnd, u):
        def two_channels(op):
            wait(e_in.at[rnd, u, op], re.at[rnd, u, op])
            spectra = dot(planes_ref[...], e_in[rnd, u, op].reshape(128, 2 * KH)).astype(BF)
            real = dot(rt[:, : 2 * KH], spectra, 1, 1)
            imag = dot(rt[:, 2 * KH :], spectra, 1, 1)
            for o2 in range(2):
                at = slice(64 * o2, 64 * o2 + 64)
                both = jnp.concatenate([real[:, at], imag[:, at]], axis=1)
                if rnd == 0:
                    both = both * column_scale(u)
                f_out[rnd, u, op, :, o2] = both.astype(BF).reshape(NQ, R, 128)
            send_plane(f_out, f_in, sf, rf, rnd, u, op)

        loop(0, 2, two_channels)

    def row_parts(rnd, kk, op):
        us = (2 * kk, 2 * kk + 1)
        for u in us:
            wait(f_in.at[rnd, u, op], rf.at[rnd, u, op])
        for o2 in range(2):
            start = pl.multiple_of((2 * op + o2) * CHUNK, CHUNK)
            part = pl.ds(start, CHUNK)
            rows_of = jnp.concatenate([f_in[rnd, u, op, :, o2].reshape(CHUNK, 128) for u in us], axis=1)
            yield start, part, pre[part] + dot(rows_of, t1t[kk * 256 : (kk + 1) * 256])

    def add_even(rnd):
        def two_channels(op):
            for _, part, total in row_parts(rnd, 0, op):
                pre[part] = total

        loop(0, 2, two_channels)

    def pointwise(rnd, lo, hi):
        field, over = ((x, 1), (slopes, 0))[rnd]

        def rows_of_one(n):
            start = pl.multiple_of(n * CHUNK, CHUNK)
            mine = expand_matrix(start)
            for i, block in mix_rows(dot(mine, lw_ref[...], 1, over).astype(BF)):
                kron[:, i * CHUNK : (i + 1) * CHUNK] = block
            part = pl.ds(start, CHUNK)
            pre[part] = dot(kron[...], field[...])
            if rnd == 0:
                pre[part] += jnp.sum(mine.astype(F32) * bias_ref[...], axis=1, keepdims=True)

        loop(lo, hi, rows_of_one)

    def widen(c):
        for kk in range(2):
            for part, wide in enumerate((w2r, w2i)):
                block = w[kk, part, c].astype(F32)
                wide[kk, c] = jnp.concatenate([block, block], axis=1)

    def mix(kk):
        wait(c_in.at[0, kk], rc.at[0, kk])
        for m in range(2):
            rows_of = c_in[0, kk, m].reshape(C, KH)
            turned[m] = (pltpu.roll(rows_of, 64, 1) * half_sign()).reshape(NQ, NI, KH)

        def terms(qq, sums):
            sums = list(sums)
            for i in range(NI):
                real = w2r[kk, 16 * i + qq]
                imag = w2i[kk, 16 * i + qq]
                for m in range(2):
                    sums[m] = sums[m] + c_in[0, kk, m, qq, i : i + 1] * real + turned[m, qq, i : i + 1] * imag
            return tuple(sums)

        sums = lax.fori_loop(0, NQ, terms, (jnp.zeros((C, KH), F32),) * 2)
        for m in range(2):
            mixed[m] = sums[m]

    def mix_back(kk):
        wait(c_in.at[1, kk], rc.at[1, kk])
        grads = []
        grads_turned = []
        for m in range(2):
            grads.append(dot(natural_ref[...], c_in[1, kk, m].reshape(C, KH).astype(BF)))
            grads_turned.append(pltpu.roll(grads[m], 64, 1) * -half_sign())
            nat[kk, m] = grads[m]

        def terms(c8):
            rows_of = ([], [])
            for n in range(8):
                c = c8 * 8 + n
                real = w2r[kk, c]
                imag = w2i[kk, c]
                for m in range(2):
                    rows_of[m].append(jnp.sum(grads[m] * real + grads_turned[m] * imag, axis=0, keepdims=True))
            for m in range(2):
                mixed[m, pl.ds(pl.multiple_of(c8 * 8, 8), 8)] = jnp.concatenate(rows_of[m], axis=0)

        loop(0, C // 8, terms)

    def transforms(rnd, last_modes, spares):
        to_owners(rnd, 0)
        last_modes(2)
        if rnd == 0:
            loop(48, C, widen)
        to_owners(rnd, 1)
        last_modes(3)
        spares(0)
        at_owners(rnd, 0)
        to_owners(rnd, 2)
        spares(1)
        at_owners(rnd, 1)
        to_owners(rnd, 3)
        spread_modes(rnd, 0)
        at_owners(rnd, 2)
        spread_modes(rnd, 1)
        at_owners(rnd, 3)
        to_rows(rnd, 0)
        spread_modes(rnd, 2)
        to_rows(rnd, 1)
        spread_modes(rnd, 3)
        to_rows(rnd, 2)
        to_rows(rnd, 3)
        spares(2)
        spares(3)
        add_even(rnd)

    def next_piece(rnd, n):
        sent_plane(a_out, sa, rnd, (n - 2) // 2, n % 2)
        send_plane(a_out, a_in, sa, ra, rnd, n // 2, n % 2)

    send_plane(a_out, a_in, sa, ra, 0, 0, 0)
    send_plane(a_out, a_in, sa, ra, 0, 0, 1)
    for i in range(NI):
        split_columns(0, i // 2, i % 2, x[i * CHUNK : (i + 1) * CHUNK], 1, NU)
    load_w.wait()
    for copy in smalls:
        copy.wait()
    next_piece(0, 2)
    loop(0, 32, widen)
    next_piece(0, 3)
    load_rows.wait()
    to_modes(0, 0, 0, 1)
    next_piece(0, 4)
    to_modes(0, 0, 1, 2)
    next_piece(0, 5)
    loop(32, 48, widen)
    to_modes(0, 1, 0, 1)
    next_piece(0, 6)
    to_modes(0, 1, 1, 2)
    next_piece(0, 7)
    load_t1t.wait()
    transforms(0, lambda u: to_modes(0, u), lambda n: pointwise(0, n, n + 1))
    copy_xm = pltpu.make_async_copy(c_in.at[0], xm_hbm, store.at[NI])
    copy_xm.start()

    load_cot.wait()

    def second(op):
        for o2, (start, part, total) in enumerate(row_parts(0, 1, op)):
            pre[part] = total

            def slab(s):
                at = pl.ds(pl.multiple_of(start + s * 16, 16), 16)
                slopes[at] = (cot[at].astype(F32) * gelu_slope(pre[at])).astype(BF)

            loop(0, CHUNK // 16, slab)
            split_columns(1, op, o2, slopes[part], 0, 1)
            send_channel(1, 0, op, o2)

    def other_quarters(op):
        for o2 in range(2):
            start = pl.multiple_of((2 * op + o2) * CHUNK, CHUNK)
            split_columns(1, op, o2, slopes[pl.ds(start, CHUNK)], 1, NU)
        send_plane(a_out, a_in, sa, ra, 1, 1, op)

    loop(0, 2, second)
    loop(0, 2, other_quarters)
    to_modes(1, 0, 0, 1)
    next_piece(1, 4)
    to_modes(1, 0, 1, 2)
    next_piece(1, 5)
    to_modes(1, 1, 0, 1)
    next_piece(1, 6)
    to_modes(1, 1, 1, 2)
    next_piece(1, 7)
    transforms(1, lambda u: to_modes(1, u), lambda n: pointwise(1, n, n + 1))
    copy_gm = pltpu.make_async_copy(nat, gm_hbm, store.at[NI + 1])
    copy_gm.start()

    def last(op):
        for o2, (_, part, total) in enumerate(row_parts(1, 1, op)):
            x[part] = total.astype(BF)
            pltpu.make_async_copy(x.at[part], sg_hbm.at[part], store.at[2 * op + o2]).start()

    loop(0, 2, last)

    for i in range(NI):
        part = pl.ds(i * CHUNK, CHUNK)
        pltpu.make_async_copy(x.at[part], sg_hbm.at[part], store.at[i]).wait()
    copy_xm.wait()
    copy_gm.wait()
    for rnd in range(2):
        for u in range(NU):
            for ip in range(2):
                sent_plane(f_out, sf, rnd, u, ip)
                wait(b_out.at[rnd, u, ip, pl.ds(0, NZ - 1)], sb.at[rnd, u, ip])
                wait(e_in.at[rnd, u, ip, pl.ds(0, NZ - 1)], se.at[rnd, u, ip])
                if u == NU - 1 or (rnd == 1 and u == 0):
                    sent_plane(a_out, sa, rnd, u, ip)
            wait(c_out.at[rnd, u, 0], sc.at[rnd, u, 1])

            @pl.when(qh != u % 2)
            def _():
                wait(c_out.at[rnd, u, 0], sc.at[rnd, u, 0])

            @pl.when(qh == u % 2)
            def _():
                wait(c_out.at[rnd, u, 0, pl.ds(0, NH - 1)], sc.at[rnd, u, 0])

        for kk in range(2):
            wait(d_out.at[rnd, kk, 0, pl.ds(0, NQ - 1)], sd.at[rnd, kk, 0])
            wait(d_out.at[rnd, kk, 0], sd.at[rnd, kk, 1])


def outputs(sg_in, xm_hbm, gm_hbm, sg_hbm, wg_hbm, xm, gm, sg, wg, xr, xi, turned, load, store_s, store_w):
    modes = [pltpu.make_async_copy(xm_hbm, xm, load.at[NI]), pltpu.make_async_copy(gm_hbm, gm, load.at[NI + 1])]
    for copy in modes:
        copy.start()
    loads, passes = [], []
    for n in range(NI):
        part = pl.ds(n * CHUNK, CHUNK)
        loads.append(pltpu.make_async_copy(sg_in.at[part], sg.at[part], load.at[n]))
        passes.append(pltpu.make_async_copy(sg.at[part], sg_hbm.at[part], store_s.at[n]))
        loads[n].start()
    low = lax.broadcasted_iota(jnp.int32, (C, KH), 1) < 64
    stores = []
    for copy in modes:
        copy.wait()
    for kk in range(2):
        for m in range(2):
            rows_of = xm[kk, m].reshape(C, KH)
            swapped = pltpu.roll(rows_of, 64, 1)
            xr[m] = jnp.where(low, rows_of, swapped).reshape(NQ, NI, KH)
            xi[m] = jnp.where(low, swapped, rows_of).reshape(NQ, NI, KH)
            turned[m] = pltpu.roll(gm[kk, m], 64, 1) * -half_sign()
        for i in range(NI):

            def terms(q4, carry):
                for n in range(4):
                    qq = q4 * 4 + n
                    total = jnp.zeros((C, KH), F32)
                    for m in range(2):
                        total = total + xr[m, qq, i : i + 1] * gm[kk, m] + xi[m, qq, i : i + 1] * turned[m]
                    wg[kk, 0, 16 * i + qq] = total[:, :64]
                    wg[kk, 1, 16 * i + qq] = total[:, 64:]
                return carry

            lax.fori_loop(0, NQ // 4, terms, 0)
            for part in range(2):
                block = (kk, part, pl.ds(16 * i, 16))
                stores.append(pltpu.make_async_copy(wg.at[block], wg_hbm.at[block], store_w.at[kk, part, i]))
                stores[-1].start()
            if kk == 0:
                loads[i].wait()
                passes[i].start()
    for store in stores + passes:
        store.wait()


def local(surface, cotangent, spectral_weight, local_weight, bias_vector):
    columns, rows = tables()
    t1 = jnp.asarray(columns, BF)
    t1t = jnp.asarray(columns.T, BF)
    row_table = jnp.asarray(rows, BF)
    gather, spread, natural, modes, planes = (jnp.asarray(p, BF) for p in permutations())
    anywhere = pl.BlockSpec(memory_space=pl.ANY)
    DMA = pltpu.SemaphoreType.DMA
    V = pltpu.VMEM
    shape = jax.ShapeDtypeStruct
    surface_gradient, xm, gm = pl.pallas_call(
        transfers,
        out_shape=(
            shape((ROWS, W), BF),
            shape((2, 2, NQ, NI, KH), F32),
            shape((2, 2, C, KH), F32),
        ),
        in_specs=[anywhere] * 13,
        out_specs=[anywhere] * 3,
        scratch_shapes=[
            V((C, C), BF),
            V((1, C), F32),
            V((32, 256), BF),
            V((64, 64), BF),
            V((64, 64), BF),
            V((32, 32), BF),
            V((128, 128), BF),
            V((ROWS, W), BF),
            V((ROWS, W), BF),
            V((2, 2, C, C, 64), BF),
            V((W, 2 * KW), BF),
            V((2 * KW, W), BF),
            V((CHUNK, 4 * KH), BF),
            V((2, C, C, KH), F32),
            V((2, C, C, KH), F32),
            V((CHUNK, ROWS), BF),
            V((ROWS, W), F32),
            V((ROWS, W), BF),
            V((2, NU, 2, NQ, 2, R, 128), BF),
            V((2, NU, 2, NQ, 2, R, 128), BF),
            V((2, NU, 2, NZ, 2 * NH, 2 * KH), BF),
            V((2, NU, 2, NZ, 2 * NH, 2 * KH), BF),
            V((2, NU, 2, NH, NI, KH), F32),
            V((2, 2, 2, NQ, NI, KH), F32),
            V((2, 2, 2, NQ, NI, KH), F32),
            V((2, NU, 2, NH, NI, KH), F32),
            V((2, NU, 2, 2 * NH, 2 * KH), BF),
            V((2, NU, 2, NZ, 2 * NH, 2 * KH), BF),
            V((2, NU, 2, NQ, 2, R, 128), BF),
            V((2, NU, 2, NQ, 2, R, 128), BF),
            V((2, NQ, NI, KH), F32),
            V((2, C, KH), F32),
            V((2, 2, C, KH), F32),
            DMA((16,)),
            DMA((NI + 2,)),
            DMA((2, NU, 2)),
            DMA((2, NU, 2)),
            DMA((2, NU, 2)),
            DMA((2, NU)),
            DMA((2, NU, 2)),
            DMA((2, 2)),
            DMA((2, 2, 2)),
            DMA((2, NU)),
            DMA((2, NU, 2)),
            DMA((2, NU, 2)),
            DMA((2, NU, 2)),
            DMA((2, NU, 2)),
        ],
        compiler_params=pltpu.CompilerParams(
            collective_id=0, has_side_effects=True, vmem_limit_bytes=56 * 1024 * 1024
        ),
        name="transfers",
    )(
        surface.reshape(ROWS, W),
        cotangent.reshape(ROWS, W),
        spectral_weight,
        t1,
        t1t,
        row_table,
        local_weight,
        bias_vector.reshape(1, C),
        gather,
        spread,
        natural,
        modes,
        planes,
    )
    surface_gradient, weight_gradient = pl.pallas_call(
        outputs,
        out_shape=(shape((ROWS, W), BF), shape((2, 2, C, C, 64), F32)),
        in_specs=[anywhere] * 3,
        out_specs=[anywhere] * 2,
        scratch_shapes=[
            V((2, 2, NQ, NI, KH), F32),
            V((2, 2, C, KH), F32),
            V((ROWS, W), BF),
            V((2, 2, C, C, 64), F32),
            V((2, NQ, NI, KH), F32),
            V((2, NQ, NI, KH), F32),
            V((2, C, KH), F32),
            DMA((NI + 2,)),
            DMA((NI,)),
            DMA((2, 2, NI)),
        ],
        compiler_params=pltpu.CompilerParams(vmem_limit_bytes=56 * 1024 * 1024),
        name="outputs",
    )(surface_gradient, xm, gm)
    return surface_gradient.reshape(1, C, R, W), weight_gradient


def solution(mesh):
    placed = (
        P("batch", None, "rows", None),
        P("batch", None, "rows", None),
        P("rows", None, None, None, "batch"),
        P(),
        P(),
    )
    return jax.shard_map(
        local,
        mesh=mesh,
        in_specs=placed,
        out_specs=(P("batch", None, "rows", None), P("rows", None, None, None, "batch")),
        check_vma=False,
    )
```
